128 devices in a mesh: seq: 32 (over x, z, y_hi), proj: 4 (over y_lo, core).
Axes of the slice: x: 4, y: 4 (y_hi: 2, y_lo: 2; y = y_hi * 2 + y_lo), z: 4, core: 2. Of those that a mesh axis runs over, the one named last changes fastest.
Arguments:
- tokens: bfloat16 [8192, 8192], P('seq', 'proj'), may hold values from -6 to 6
- value_weight: bfloat16 [8192, 4096], P('proj'), may hold values from -0.0625 to 0.0625
- query: bfloat16 [8192, 4096], P('seq', 'proj'), may hold values from -6 to 6
- keyed: bfloat16 [8192, 4096], P('seq', 'proj'), may hold values from -6 to 6
- filters: float32 [8192, 4096], P('seq', 'proj'), may hold values from -2 to 2
- skip_gain: float32 [4096], P('proj'), may hold values from -4 to 4
Outputs:
- mixed_out: bfloat16 [8192, 4096], P('seq', 'proj')
The draws below stay inside these ranges and needn't reach their ends.
All inputs are finite; a program needn't handle non-finite values.
Results may differ from the reference program's by a relative error of at most 0.0017.
Values sent between devices are 32-bit elements; how exact they have to be, the bound alone decides.
A program may use at most 128 MiB of HBM per device.

```python
import math
import jax
import jax.numpy as jnp

WIDTH = 8192
CHANNELS = 4096
LENGTH = 8192
FFT_LEN = 16384


def draw_filters(key, part):
    key = jax.random.fold_in(key, 7)
    noise_key, decay_key = jax.random.split(key)
    lowest = 32.0
    noise = jnp.clip(jax.random.normal(noise_key, (LENGTH, CHANNELS), jnp.float32), -6.0, 6.0)
    highest = 4.0 * LENGTH
    spans = jnp.exp(jax.random.uniform(decay_key, (CHANNELS,), jnp.float32, math.log(lowest), math.log(highest)))
    taps = jnp.arange(LENGTH, dtype=jnp.float32)[:, None]
    return noise * jnp.sqrt(2.0 / spans) * jnp.exp(-taps / spans)


def steps_of(own_key, shape, shards, low, high):
    factor_of = 1.0
    for dim, parts in shards:
        heights = jax.random.uniform(jax.random.fold_in(jax.random.fold_in(own_key, 6), dim), (parts,), jnp.float32, low / len(shards), high / len(shards))
        factor_of = factor_of * jnp.repeat(jnp.exp(heights), shape[dim] // parts).reshape((-1,) + (1,) * (len(shape) - 1 - dim))
    return factor_of


def normal_values(own_key, dims, scale, bound, pieces=(), kind=jnp.bfloat16):
    array = jax.random.normal(own_key, dims, jnp.float32) * scale
    if len(pieces) > 0:
        array = steps_of(own_key, dims, pieces, -0.22, 0.18) * array
    return jnp.clip(array, min=-bound, max=bound).astype(kind)


def setup_inputs(seed: int = 0) -> dict:
    key_list = jax.random.split(jax.random.key(seed), 7)
    tokens = normal_values(key_list[0], (LENGTH, WIDTH), 1.0, 6.0, ((0, 32), (1, 4)))
    value_weight = normal_values(key_list[1], (WIDTH, CHANNELS), WIDTH ** -0.5, 0.0625, ((0, 4),))
    query = normal_values(key_list[2], (LENGTH, CHANNELS), 1.0, 6.0, ((0, 32), (1, 4)))
    keyed = normal_values(key_list[3], (LENGTH, CHANNELS), 1.0, 6.0, ((0, 32), (1, 4)))
    filters = draw_filters(jax.random.fold_in(key_list[6], 71), 0)
    skip_gain = normal_values(key_list[5], (CHANNELS,), 1.0, 4.0, ((0, 4),), jnp.float32)
    return {"tokens": tokens, "value_weight": value_weight, "query": query, "keyed": keyed, "filters": filters, "skip_gain": skip_gain}


def reference(tokens, value_weight, query, keyed, filters, skip_gain):
    valued = jnp.dot(tokens, value_weight, preferred_element_type=jnp.float32)
    gated = keyed.astype(jnp.float32) * valued
    spectrum = jnp.fft.rfft(gated, n=FFT_LEN, axis=0) * jnp.fft.rfft(filters, n=FFT_LEN, axis=0)
    conv = jnp.fft.irfft(spectrum, n=FFT_LEN, axis=0)[:LENGTH]
    return (query.astype(jnp.float32) * (conv + skip_gain * gated)).astype(jnp.bfloat16)
```

```python
import functools

import jax
import jax.numpy as jnp
import ml_dtypes
import numpy as np
from jax import lax
from jax.experimental import pallas as pl
from jax.experimental.pallas import tpu as pltpu
from jax.sharding import PartitionSpec as P

MESH = pl.DeviceIdType.MESH
F32 = jnp.float32
BF16 = jnp.bfloat16
SUB = 8


def odd_tables(block):
    n = np.arange(block)
    k = np.arange(block)
    angle = np.pi / (2 * block) * ((n[:, None] * (2 * k[None, :] + 1)) % (4 * block))
    forward = np.concatenate([np.cos(angle), -np.sin(angle)], axis=1)
    inverse = forward.T / block

    def split(table):
        high = table.astype(np.float32).astype(ml_dtypes.bfloat16)
        low = (table - high.astype(np.float64)).astype(np.float32).astype(ml_dtypes.bfloat16)
        return high, low

    return split(forward) + split(inverse)


def split_rows(values):
    high = values.astype(BF16)
    low = (values - high.astype(F32)).astype(BF16)
    return high, low


def dot(a, b):
    return jnp.dot(a, b, preferred_element_type=F32)


def table_dot(values, table_high, table_low):
    rows = values.shape[0]
    high, low = split_rows(values)
    both = dot(jnp.concatenate([high, low], axis=0), table_high)
    return both[:rows] + both[rows:] + dot(high, table_low)


def kernel(
    seq_count, chunks,
    tokens_h, weight_h, query_h, keyed_h, filters_h, skip_v, fwd_high_h, fwd_low_h, inv_high_h, inv_low_h,
    out_h,
    tokens_v, weight_v, query_v, keyed_v, filters_v, fwd_high, fwd_low, inv_high, inv_low,
    near_send, near_recv, far_send, far_recv, own_far, own_near, gated_v,
    filt_send, filt_recv, sig_send, sig_recv, back_send, back_recv, out_v,
    filt_spec, sig_spec, prod_spec,
    load_sem, weight_sem, near_send_sem, near_recv_sem, far_send_sem, far_recv_sem,
    filt_send_sem, filt_recv_sem, sig_send_sem, sig_recv_sem, back_send_sem, back_recv_sem, out_sem,
):
    seq = lax.axis_index("seq")
    proj = lax.axis_index("proj")
    core = lax.rem(proj, 2)
    side = proj // 2
    core_partner = side * 2 + 1 - core
    chip_partner = (1 - side) * 2 + core
    rows = tokens_h.shape[0]
    width = skip_v.shape[1]
    step = width // chunks
    blocks = seq_count // 2
    block = 2 * rows

    def columns(start):
        return pl.ds(pl.multiple_of(start, step), step)

    filter_load = pltpu.make_async_copy(filters_h, filters_v, load_sem.at[0])
    token_load = pltpu.make_async_copy(tokens_h, tokens_v, load_sem.at[1])
    filter_load.start()
    token_load.start()
    quarters = ((1 - side) * 2 + 1 - core, (1 - side) * 2 + core, side * 2 + 1 - core, side * 2 + core)

    def weight_load(quarter, n):
        slot = quarter * chunks + n
        return pltpu.make_async_copy(
            weight_h.at[:, columns(quarters[quarter] * width + n * step)], weight_v.at[slot], weight_sem.at[slot]
        )

    for pair in range(2):
        for n in range(chunks):
            weight_load(2 * pair, n).start()
            weight_load(2 * pair + 1, n).start()
    table_loads = [
        pltpu.make_async_copy(src, dst, load_sem.at[2 + i])
        for i, (src, dst) in enumerate(
            ((fwd_high_h, fwd_high), (fwd_low_h, fwd_low), (inv_high_h, inv_high), (inv_low_h, inv_low))
        )
    ]
    for copy in table_loads:
        copy.start()
    part_loads = []
    for n in range(chunks):
        part_loads.append(pltpu.make_async_copy(keyed_h.at[:, pl.ds(n * step, step)], keyed_v.at[n], load_sem.at[6 + n]))
        part_loads.append(
            pltpu.make_async_copy(query_h.at[:, pl.ds(n * step, step)], query_v.at[n], load_sem.at[6 + chunks + n])
        )
    for copy in part_loads:
        copy.start()

    barrier = pltpu.get_barrier_semaphore()

    def greet(d, carry):
        peer = lax.rem(seq + d, seq_count)
        pl.semaphore_signal(barrier, inc=1, device_id=(peer, proj), device_id_type=MESH)
        return carry

    lax.fori_loop(1, seq_count, greet, 0)
    for partner in (core_partner, chip_partner):
        pl.semaphore_signal(barrier, inc=1, device_id=(seq, partner), device_id_type=MESH)
    pl.semaphore_wait(barrier, seq_count + 1)

    def spread(source, target, send_sem, recv_sem):
        def send(d, carry):
            peer = lax.rem(seq + d, seq_count)
            pltpu.make_async_remote_copy(
                src_ref=source(peer), dst_ref=target(seq), send_sem=send_sem, recv_sem=recv_sem,
                device_id=(peer, proj), device_id_type=MESH,
            ).start()
            return carry

        pltpu.make_async_copy(source(seq), target(seq), recv_sem).start()
        lax.fori_loop(1, seq_count, send, 0)

    def await_bytes(ref, sem):
        pltpu.make_async_copy(ref, ref, sem).wait()

    filter_load.wait()

    def send_filters(n, carry):
        part = filters_v[:, columns(n * step)].T
        filt_send[:, pl.ds(n, 1)] = part.reshape(seq_count, 1, SUB, rows)
        return carry

    lax.fori_loop(0, chunks, send_filters, 0)
    spread(lambda r: filt_send.at[r], lambda r: filt_recv.at[r], filt_send_sem, filt_recv_sem)

    token_load.wait()

    def project(quarter, n):
        weight_load(quarter, n).wait()
        return dot(tokens_v[...], weight_v[quarter * chunks + n])

    def near_copy(pair, n):
        return pltpu.make_async_remote_copy(
            src_ref=near_send.at[pair, n], dst_ref=near_recv.at[pair, n],
            send_sem=near_send_sem.at[pair, n], recv_sem=near_recv_sem.at[pair, n],
            device_id=(seq, core_partner), device_id_type=MESH,
        )

    def far_copy(n):
        return pltpu.make_async_remote_copy(
            src_ref=far_send.at[n], dst_ref=far_recv.at[n],
            send_sem=far_send_sem.at[n], recv_sem=far_recv_sem.at[n],
            device_id=(seq, chip_partner), device_id_type=MESH,
        )

    def send_far(n):
        near_copy(0, n).wait_recv()
        far_send[n] = own_far[n] + near_recv[0, n]
        far_copy(n).start()

    def project_far(n, carry):
        near_send[0, n] = project(0, n)
        near_copy(0, n).start()
        own_far[n] = project(1, n)

        @pl.when(n > 0)
        def _():
            send_far(n - 1)

        return carry

    lax.fori_loop(0, chunks, project_far, 0)
    send_far(chunks - 1)

    def project_near(n, carry):
        near_send[1, n] = project(2, n)
        near_copy(1, n).start()
        own_near[n] = project(3, n)
        return carry

    lax.fori_loop(0, chunks, project_near, 0)

    for copy in table_loads:
        copy.wait()
    await_bytes(filt_recv, filt_recv_sem)
    flip = (1 - 2 * lax.rem(lax.broadcasted_iota(jnp.int32, (1, 1, block), 2), 2)).astype(F32)

    def block_spectra(values):
        pairs = values.reshape(blocks, 2, SUB, rows)
        joined = jnp.concatenate([pairs[:, 0], pairs[:, 1]], axis=2).reshape(blocks * SUB, block)
        return table_dot(joined, fwd_high[...], fwd_low[...]).reshape(blocks, SUB, 2 * block)

    def filter_spectra(n, carry):
        spec = block_spectra(filt_recv[:, pl.ds(n, 1)].reshape(seq_count, SUB, rows))
        filt_spec[n] = spec
        filt_spec[n, 1:, :, :block] = spec[1:, :, :block] - flip * spec[:-1, :, block:]
        filt_spec[n, 1:, :, block:] = spec[1:, :, block:] + flip * spec[:-1, :, :block]
        return carry

    lax.fori_loop(0, chunks, filter_spectra, 0)
    for copy in part_loads:
        copy.wait()

    def gate(n):
        near_copy(1, n).wait_recv()
        far_copy(n).wait_recv()
        valued = own_near[n] + near_recv[1, n] + far_recv[n]
        gated = keyed_v[n].astype(F32) * valued
        gated_v[n] = gated
        sig_send[n] = gated.T.reshape(seq_count, SUB, rows)
        spread(
            lambda r: sig_send.at[n, r], lambda r: sig_recv.at[n, r], sig_send_sem.at[n], sig_recv_sem.at[n]
        )

    def convolve(n):
        await_bytes(sig_recv.at[n], sig_recv_sem.at[n])
        sig_spec[...] = block_spectra(sig_recv[n])

        def lanes(part, carry):
            re = pl.ds(pl.multiple_of(part * 128, 128), 128)
            im = pl.ds(pl.multiple_of(block + part * 128, 128), 128)
            sig_re = [sig_spec[j, :, re] for j in range(blocks)]
            sig_im = [sig_spec[j, :, im] for j in range(blocks)]
            for s in range(blocks):
                sum_re = sum_im = None
                for j in range(s + 1):
                    tap_re, tap_im = filt_spec[n, j, :, re], filt_spec[n, j, :, im]
                    x_re, x_im = sig_re[s - j], sig_im[s - j]
                    term_re = tap_re * x_re - tap_im * x_im
                    term_im = tap_re * x_im + tap_im * x_re
                    sum_re = term_re if sum_re is None else sum_re + term_re
                    sum_im = term_im if sum_im is None else sum_im + term_im
                prod_spec[s, :, re] = sum_re
                prod_spec[s, :, im] = sum_im
            return carry

        lax.fori_loop(0, block // 128, lanes, 0)
        result = table_dot(
            prod_spec[...].reshape(blocks * SUB, 2 * block), inv_high[...], inv_low[...]
        ).reshape(blocks, SUB, block)
        pairs = jnp.stack([result[:, :, :rows], result[:, :, rows:]], axis=1)
        back_send[n] = pairs.reshape(seq_count, SUB, rows)
        spread(
            lambda r: back_send.at[n, r], lambda r: back_recv.at[n, r], back_send_sem.at[n], back_recv_sem.at[n]
        )

    def out_copy(n):
        return pltpu.make_async_copy(out_v.at[n], out_h.at[:, columns(n * step)], out_sem.at[n])

    def finish(n):
        await_bytes(back_recv.at[n], back_recv_sem.at[n])
        conv = back_recv[n].reshape(step, rows).T
        skip = skip_v[:, columns(n * step)]
        out_v[n] = (query_v[n].astype(F32) * (conv + skip * gated_v[n])).astype(BF16)
        out_copy(n).start()

    def stage(i, carry):
        @pl.when(i < chunks)
        def _():
            gate(i)

        @pl.when(jnp.logical_and(i >= 1, i <= chunks))
        def _():
            convolve(i - 1)

        @pl.when(i >= 2)
        def _():
            finish(i - 2)

        return carry

    lax.fori_loop(0, chunks + 2, stage, 0)

    def drain(n, carry):
        near_copy(0, n).wait_send()
        near_copy(1, n).wait_send()
        far_copy(n).wait_send()
        await_bytes(sig_send.at[n, pl.ds(0, seq_count - 1)], sig_send_sem.at[n])
        await_bytes(back_send.at[n, pl.ds(0, seq_count - 1)], back_send_sem.at[n])
        out_copy(n).wait()
        return carry

    await_bytes(filt_send.at[pl.ds(0, seq_count - 1)], filt_send_sem)
    lax.fori_loop(0, chunks, drain, 0)


def body(seq_count, tokens, value_weight, query, keyed, filters, skip_gain):
    rows, depth = tokens.shape
    width = skip_gain.shape[0]
    chunks = width // (seq_count * SUB)
    step = width // chunks
    block = 2 * rows
    blocks = seq_count // 2
    tables = [jnp.asarray(table) for table in odd_tables(block)]
    any_space = pl.BlockSpec(memory_space=pl.ANY)
    dma = pltpu.SemaphoreType.DMA
    strip = pltpu.VMEM((chunks, rows, step), F32)
    pieces = pltpu.VMEM((chunks, seq_count, SUB, rows), F32)
    filt_pieces = pltpu.VMEM((seq_count, chunks, SUB, rows), F32)
    return pl.pallas_call(
        functools.partial(kernel, seq_count, chunks),
        out_shape=jax.ShapeDtypeStruct((rows, width), BF16),
        in_specs=[any_space] * 5 + [pl.BlockSpec(memory_space=pltpu.VMEM)] + [any_space] * 4,
        out_specs=any_space,
        scratch_shapes=[
            pltpu.VMEM((rows, depth), BF16),
            pltpu.VMEM((4 * chunks, depth, step), BF16),
            pltpu.VMEM((chunks, rows, step), BF16),
            pltpu.VMEM((chunks, rows, step), BF16),
            pltpu.VMEM((rows, width), F32),
            pltpu.VMEM((block, 2 * block), BF16),
            pltpu.VMEM((block, 2 * block), BF16),
            pltpu.VMEM((2 * block, block), BF16),
            pltpu.VMEM((2 * block, block), BF16),
            pltpu.VMEM((2, chunks, rows, step), F32),
            pltpu.VMEM((2, chunks, rows, step), F32),
            strip, strip, strip, strip, strip,
            filt_pieces, filt_pieces, pieces, pieces, pieces, pieces,
            pltpu.VMEM((chunks, rows, step), BF16),
            pltpu.VMEM((chunks, blocks, SUB, 2 * block), F32),
            pltpu.VMEM((blocks, SUB, 2 * block), F32),
            pltpu.VMEM((blocks, SUB, 2 * block), F32),
            dma((6 + 2 * chunks,)), dma((4 * chunks,)),
            dma((2, chunks)), dma((2, chunks)), dma((chunks,)), dma((chunks,)),
            dma, dma, dma((chunks,)), dma((chunks,)), dma((chunks,)), dma((chunks,)), dma((chunks,)),
        ],
        compiler_params=pltpu.CompilerParams(
            collective_id=0, has_side_effects=True, vmem_limit_bytes=56 * 1024 * 1024
        ),
    )(tokens, value_weight, query, keyed, filters, skip_gain.reshape(1, width), *tables)


def solution(mesh):
    in_specs = (
        P("seq", "proj"),
        P("proj", None),
        P("seq", "proj"),
        P("seq", "proj"),
        P("seq", "proj"),
        P("proj"),
    )
    return jax.shard_map(
        functools.partial(body, mesh.shape["seq"]), mesh=mesh, in_specs=in_specs, out_specs=P("seq", "proj"), check_vma=False
    )
```

```python
import functools
import math

import jax
import jax.numpy as jnp
import ml_dtypes
import numpy as np
from jax import lax
from jax.experimental import pallas as pl
from jax.experimental.pallas import tpu as pltpu
from jax.sharding import PartitionSpec as P

MESH = pl.DeviceIdType.MESH
F32 = jnp.float32
BF16 = jnp.bfloat16
SUB = 8
LAG = 4


def odd_tables(block):
    n = np.arange(block)
    k = np.arange(block)
    angle = np.pi / (2 * block) * ((n[:, None] * (2 * k[None, :] + 1)) % (4 * block))
    forward = np.concatenate([np.cos(angle), -np.sin(angle)], axis=1)
    inverse = forward.T / block

    def split(table):
        high = table.astype(np.float32).astype(ml_dtypes.bfloat16)
        low = (table - high.astype(np.float64)).astype(np.float32).astype(ml_dtypes.bfloat16)
        return high, low

    return split(forward) + split(inverse)


def split_rows(values):
    high = values.astype(BF16)
    low = (values - high.astype(F32)).astype(BF16)
    return high, low


def dot(a, b):
    return jnp.dot(a, b, preferred_element_type=F32)


def table_dot(values, table_high, table_low):
    rows = values.shape[0]
    high, low = split_rows(values)
    both = dot(jnp.concatenate([high, low], axis=0), table_high)
    return both[:rows] + both[rows:] + dot(high, table_low)


def kernel(
    edge, seq_count, chunks,
    tokens_h, weight_h, query_h, keyed_h, filters_h, skip_v, fwd_high_h, fwd_low_h, inv_high_h, inv_low_h,
    out_h,
    tokens_v, weight_v, query_v, keyed_v, filters_v, fwd_high, fwd_low, inv_high, inv_low,
    near_send, near_recv, far_send, far_recv, own_far, own_near, gated_v,
    filt_send, filt_recv, sig_send, sig_recv, back_send, back_recv, out_v,
    filt_spec, sig_spec, prod_spec,
    load_sem, weight_sem, near_send_sem, near_recv_sem, far_send_sem, far_recv_sem,
    filt_send_sem, filt_recv_sem, sig_send_sem, sig_recv_sem, back_send_sem, back_recv_sem, out_sem, round_sem,
):
    seq = lax.axis_index("seq")
    proj = lax.axis_index("proj")
    core = lax.rem(proj, 2)
    side = proj // 2
    core_partner = side * 2 + 1 - core
    chip_partner = (1 - side) * 2 + core
    rows = tokens_h.shape[0]
    width = skip_v.shape[1]
    step = width // chunks
    blocks = seq_count // 2
    block = 2 * rows

    def columns(start):
        return pl.ds(pl.multiple_of(start, step), step)

    filter_load = pltpu.make_async_copy(filters_h, filters_v, load_sem.at[0])
    token_load = pltpu.make_async_copy(tokens_h, tokens_v, load_sem.at[1])
    filter_load.start()
    token_load.start()
    quarters = ((1 - side) * 2 + 1 - core, (1 - side) * 2 + core, side * 2 + 1 - core, side * 2 + core)

    def weight_load(quarter, n):
        slot = quarter * chunks + n
        return pltpu.make_async_copy(
            weight_h.at[:, columns(quarters[quarter] * width + n * step)], weight_v.at[slot], weight_sem.at[slot]
        )

    for pair in range(2):
        for n in range(chunks):
            weight_load(2 * pair, n).start()
            weight_load(2 * pair + 1, n).start()
    table_loads = [
        pltpu.make_async_copy(src, dst, load_sem.at[2 + i])
        for i, (src, dst) in enumerate(
            ((fwd_high_h, fwd_high), (fwd_low_h, fwd_low), (inv_high_h, inv_high), (inv_low_h, inv_low))
        )
    ]
    for copy in table_loads:
        copy.start()
    part_loads = []
    for n in range(chunks):
        part_loads.append(pltpu.make_async_copy(keyed_h.at[:, pl.ds(n * step, step)], keyed_v.at[n], load_sem.at[6 + n]))
        part_loads.append(
            pltpu.make_async_copy(query_h.at[:, pl.ds(n * step, step)], query_v.at[n], load_sem.at[6 + chunks + n])
        )
    for copy in part_loads:
        copy.start()

    row, column, half = seq // (2 * edge), lax.rem(seq // 2, edge), lax.rem(seq, 2)

    def place(d):
        return (
            lax.rem(row + d // (2 * edge), edge) * edge + lax.rem(column + lax.rem(d // 2, edge), edge)
        ) * 2 + lax.rem(half + lax.rem(d, 2), 2)

    barrier = pltpu.get_barrier_semaphore()

    def greet(sem, peer, part):
        pl.semaphore_signal(sem, inc=1, device_id=(peer, part), device_id_type=MESH)

    for d in range(1, edge):
        greet(barrier, place(2 * d), proj)
        greet(barrier, place(2 * edge * d), proj)
    greet(barrier, place(1), proj)
    greet(barrier, seq, core_partner)
    greet(barrier, seq, chip_partner)

    def spread(source, target, send_sem, recv_sem):
        def send(d, carry):
            peer = place(d)
            pltpu.make_async_remote_copy(
                src_ref=source(peer), dst_ref=target(seq), send_sem=send_sem, recv_sem=recv_sem,
                device_id=(peer, proj), device_id_type=MESH,
            ).start()
            return carry

        pltpu.make_async_copy(source(seq), target(seq), recv_sem).start()
        lax.fori_loop(1, seq_count, send, 0)

    def await_bytes(ref, sem):
        pltpu.make_async_copy(ref, ref, sem).wait()

    token_load.wait()

    def project(quarter, n):
        weight_load(quarter, n).wait()
        return dot(tokens_v[...], weight_v[quarter * chunks + n])

    def near_copy(pair, n):
        return pltpu.make_async_remote_copy(
            src_ref=near_send.at[pair, n], dst_ref=near_recv.at[pair, n],
            send_sem=near_send_sem.at[pair, n], recv_sem=near_recv_sem.at[pair, n],
            device_id=(seq, core_partner), device_id_type=MESH,
        )

    def far_copy(n):
        return pltpu.make_async_remote_copy(
            src_ref=far_send.at[n], dst_ref=far_recv.at[n],
            send_sem=far_send_sem.at[n], recv_sem=far_recv_sem.at[n],
            device_id=(seq, chip_partner), device_id_type=MESH,
        )

    def send_far(n):
        near_copy(0, n).wait_recv()
        far_send[n] = own_far[n] + near_recv[0, n]
        far_copy(n).start()

    def project_far(n):
        near_send[0, n] = project(0, n)
        near_copy(0, n).start()
        own_far[n] = project(1, n)

    near_send[0, 0] = project(0, 0)
    own_far[0] = project(1, 0)
    pl.semaphore_wait(barrier, 2 * edge + 1)
    near_copy(0, 0).start()
    for d in range(1, edge):
        greet(round_sem.at[0], place(2 * d), proj)
    project_far(1)
    pl.semaphore_wait(round_sem.at[0], edge - 1)
    greet(round_sem.at[1], place(1), proj)
    send_far(0)
    project_far(2)
    send_far(1)
    pl.semaphore_wait(round_sem.at[1], 1)

    filter_load.wait()

    def send_filters(n, carry):
        part = filters_v[:, columns(n * step)].T
        filt_send[:, pl.ds(n, 1)] = part.reshape(seq_count, 1, SUB, rows)
        return carry

    lax.fori_loop(0, chunks, send_filters, 0)
    spread(lambda r: filt_send.at[r], lambda r: filt_recv.at[r], filt_send_sem, filt_recv_sem)


    def project_rest(n, carry):
        project_far(n)
        send_far(n - 1)
        return carry

    lax.fori_loop(3, chunks, project_rest, 0)
    send_far(chunks - 1)

    def project_near(n, carry):
        near_send[1, n] = project(2, n)
        near_copy(1, n).start()
        own_near[n] = project(3, n)
        return carry

    lax.fori_loop(0, chunks, project_near, 0)

    for copy in table_loads:
        copy.wait()
    await_bytes(filt_recv, filt_recv_sem)
    flip = (1 - 2 * lax.rem(lax.broadcasted_iota(jnp.int32, (1, 1, block), 2), 2)).astype(F32)

    def block_spectra(values):
        pairs = values.reshape(blocks, 2, SUB, rows)
        joined = jnp.concatenate([pairs[:, 0], pairs[:, 1]], axis=2).reshape(blocks * SUB, block)
        return table_dot(joined, fwd_high[...], fwd_low[...]).reshape(blocks, SUB, 2 * block)

    def filter_spectra(n, carry):
        spec = block_spectra(filt_recv[:, pl.ds(n, 1)].reshape(seq_count, SUB, rows))
        filt_spec[n] = spec
        filt_spec[n, 1:, :, :block] = spec[1:, :, :block] - flip * spec[:-1, :, block:]
        filt_spec[n, 1:, :, block:] = spec[1:, :, block:] + flip * spec[:-1, :, :block]
        return carry

    lax.fori_loop(0, chunks, filter_spectra, 0)
    for copy in part_loads:
        copy.wait()

    def gate(n):
        near_copy(1, n).wait_recv()
        far_copy(n).wait_recv()
        valued = own_near[n] + near_recv[1, n] + far_recv[n]
        gated = keyed_v[n].astype(F32) * valued
        gated_v[n] = gated
        sig_send[n] = gated.T.reshape(seq_count, SUB, rows)
        spread(
            lambda r: sig_send.at[n, r], lambda r: sig_recv.at[n, r], sig_send_sem.at[n], sig_recv_sem.at[n]
        )

    def convolve(n):
        await_bytes(sig_recv.at[n], sig_recv_sem.at[n])
        sig_spec[...] = block_spectra(sig_recv[n])

        def lanes(part, carry):
            re = pl.ds(pl.multiple_of(part * 128, 128), 128)
            im = pl.ds(pl.multiple_of(block + part * 128, 128), 128)
            sig_re = [sig_spec[j, :, re] for j in range(blocks)]
            sig_im = [sig_spec[j, :, im] for j in range(blocks)]
            for s in range(blocks):
                sum_re = sum_im = None
                for j in range(s + 1):
                    tap_re, tap_im = filt_spec[n, j, :, re], filt_spec[n, j, :, im]
                    x_re, x_im = sig_re[s - j], sig_im[s - j]
                    term_re = tap_re * x_re - tap_im * x_im
                    term_im = tap_re * x_im + tap_im * x_re
                    sum_re = term_re if sum_re is None else sum_re + term_re
                    sum_im = term_im if sum_im is None else sum_im + term_im
                prod_spec[s, :, re] = sum_re
                prod_spec[s, :, im] = sum_im
            return carry

        lax.fori_loop(0, block // 128, lanes, 0)
        result = table_dot(
            prod_spec[...].reshape(blocks * SUB, 2 * block), inv_high[...], inv_low[...]
        ).reshape(blocks, SUB, block)
        pairs = jnp.stack([result[:, :, :rows], result[:, :, rows:]], axis=1)
        back_send[n] = pairs.reshape(seq_count, SUB, rows)
        spread(
            lambda r: back_send.at[n, r], lambda r: back_recv.at[n, r], back_send_sem.at[n], back_recv_sem.at[n]
        )

    def out_copy(n):
        return pltpu.make_async_copy(out_v.at[n], out_h.at[:, columns(n * step)], out_sem.at[n])

    def finish(n):
        await_bytes(back_recv.at[n], back_recv_sem.at[n])
        conv = back_recv[n].reshape(step, rows).T
        skip = skip_v[:, columns(n * step)]
        out_v[n] = (query_v[n].astype(F32) * (conv + skip * gated_v[n])).astype(BF16)
        out_copy(n).start()

    def stage(i, carry):
        @pl.when(i < chunks)
        def _():
            gate(i)

        @pl.when(i >= LAG)
        def _():
            convolve(i - LAG)

        return carry

    lax.fori_loop(0, chunks + LAG, stage, 0)

    def last(n, carry):
        finish(n)
        return carry

    lax.fori_loop(0, chunks, last, 0)

    def drain(n, carry):
        near_copy(0, n).wait_send()
        near_copy(1, n).wait_send()
        far_copy(n).wait_send()
        await_bytes(sig_send.at[n, pl.ds(0, seq_count - 1)], sig_send_sem.at[n])
        await_bytes(back_send.at[n, pl.ds(0, seq_count - 1)], back_send_sem.at[n])
        out_copy(n).wait()
        return carry

    await_bytes(filt_send.at[pl.ds(0, seq_count - 1)], filt_send_sem)
    lax.fori_loop(0, chunks, drain, 0)


def body(seq_count, tokens, value_weight, query, keyed, filters, skip_gain):
    rows, depth = tokens.shape
    width = skip_gain.shape[0]
    chunks = width // (seq_count * SUB)
    step = width // chunks
    block = 2 * rows
    blocks = seq_count // 2
    tables = [jnp.asarray(table) for table in odd_tables(block)]
    any_space = pl.BlockSpec(memory_space=pl.ANY)
    dma = pltpu.SemaphoreType.DMA
    strip = pltpu.VMEM((chunks, rows, step), F32)
    pieces = pltpu.VMEM((chunks, seq_count, SUB, rows), F32)
    filt_pieces = pltpu.VMEM((seq_count, chunks, SUB, rows), F32)
    return pl.pallas_call(
        functools.partial(kernel, math.isqrt(seq_count // 2), seq_count, chunks),
        out_shape=jax.ShapeDtypeStruct((rows, width), BF16),
        in_specs=[any_space] * 5 + [pl.BlockSpec(memory_space=pltpu.VMEM)] + [any_space] * 4,
        out_specs=any_space,
        scratch_shapes=[
            pltpu.VMEM((rows, depth), BF16),
            pltpu.VMEM((4 * chunks, depth, step), BF16),
            pltpu.VMEM((chunks, rows, step), BF16),
            pltpu.VMEM((chunks, rows, step), BF16),
            pltpu.VMEM((rows, width), F32),
            pltpu.VMEM((block, 2 * block), BF16),
            pltpu.VMEM((block, 2 * block), BF16),
            pltpu.VMEM((2 * block, block), BF16),
            pltpu.VMEM((2 * block, block), BF16),
            pltpu.VMEM((2, chunks, rows, step), F32),
            pltpu.VMEM((2, chunks, rows, step), F32),
            strip, strip, strip, strip, strip,
            filt_pieces, filt_pieces, pieces, pieces, pieces, pieces,
            pltpu.VMEM((chunks, rows, step), BF16),
            pltpu.VMEM((chunks, blocks, SUB, 2 * block), F32),
            pltpu.VMEM((blocks, SUB, 2 * block), F32),
            pltpu.VMEM((blocks, SUB, 2 * block), F32),
            dma((6 + 2 * chunks,)), dma((4 * chunks,)),
            dma((2, chunks)), dma((2, chunks)), dma((chunks,)), dma((chunks,)),
            dma, dma, dma((chunks,)), dma((chunks,)), dma((chunks,)), dma((chunks,)), dma((chunks,)),
            pltpu.SemaphoreType.REGULAR((2,)),
        ],
        compiler_params=pltpu.CompilerParams(
            collective_id=0, has_side_effects=True, vmem_limit_bytes=56 * 1024 * 1024
        ),
    )(tokens, value_weight, query, keyed, filters, skip_gain.reshape(1, width), *tables)


def solution(mesh):
    in_specs = (
        P("seq", "proj"),
        P("proj", None),
        P("seq", "proj"),
        P("seq", "proj"),
        P("seq", "proj"),
        P("proj"),
    )
    return jax.shard_map(
        functools.partial(body, mesh.shape["seq"]), mesh=mesh, in_specs=in_specs, out_specs=P("seq", "proj"), check_vma=False
    )
```

```python
import functools
import math

import jax
import jax.numpy as jnp
import ml_dtypes
import numpy as np
from jax import lax
from jax.experimental import pallas as pl
from jax.experimental.pallas import tpu as pltpu
from jax.sharding import PartitionSpec as P

MESH = pl.DeviceIdType.MESH
F32 = jnp.float32
BF16 = jnp.bfloat16
SUB = 8
EAGER = True
SPEC_AT = 0
LAG = 4


def odd_tables(block):
    n = np.arange(block)
    k = np.arange(block)
    angle = np.pi / (2 * block) * ((n[:, None] * (2 * k[None, :] + 1)) % (4 * block))
    forward = np.concatenate([np.cos(angle), -np.sin(angle)], axis=1)
    inverse = forward.T / block

    def split(table):
        high = table.astype(np.float32).astype(ml_dtypes.bfloat16)
        low = (table - high.astype(np.float64)).astype(np.float32).astype(ml_dtypes.bfloat16)
        return high, low

    return split(forward) + split(inverse)


def split_rows(values):
    high = values.astype(BF16)
    low = (values - high.astype(F32)).astype(BF16)
    return high, low


def dot(a, b):
    return jnp.dot(a, b, preferred_element_type=F32)


def table_dot(values, table_high, table_low):
    rows = values.shape[0]
    high, low = split_rows(values)
    both = dot(jnp.concatenate([high, low], axis=0), table_high)
    return both[:rows] + both[rows:] + dot(high, table_low)


def kernel(
    edge, seq_count, chunks,
    tokens_h, weight_h, query_h, keyed_h, filters_h, skip_v, fwd_high_h, fwd_low_h, inv_high_h, inv_low_h,
    out_h,
    tokens_v, weight_v, query_v, keyed_v, filters_v, fwd_high, fwd_low, inv_high, inv_low,
    partial_v, near_recv, far_send, far_recv, gated_v,
    filt_send, filt_recv, sig_send, sig_recv, back_send, back_recv, out_v,
    filt_spec, sig_spec, prod_spec,
    load_sem, weight_sem, near_send_sem, near_recv_sem, far_send_sem, far_recv_sem,
    filt_send_sem, filt_recv_sem, sig_send_sem, sig_recv_sem, back_send_sem, back_recv_sem, out_sem, round_sem,
):
    seq = lax.axis_index("seq")
    proj = lax.axis_index("proj")
    core = lax.rem(proj, 2)
    side = proj // 2
    core_partner = side * 2 + 1 - core
    chip_partner = (1 - side) * 2 + core
    rows = tokens_h.shape[0]
    width = skip_v.shape[1]
    step = width // chunks
    blocks = seq_count // 2
    block = 2 * rows

    def columns(start):
        return pl.ds(pl.multiple_of(start, step), step)

    filter_load = pltpu.make_async_copy(filters_h, filters_v, load_sem.at[0])
    token_load = pltpu.make_async_copy(tokens_h, tokens_v, load_sem.at[1])
    token_load.start()

    def weight_load(k):
        pair, inner = k // (2 * chunks), lax.rem(k, 2 * chunks)
        home_side = side + (1 - pair) * (1 - 2 * side)
        home_core = core + (1 - lax.rem(inner, 2)) * (1 - 2 * core)
        start = (home_side * 2 + home_core) * width + inner // 2 * step
        return pltpu.make_async_copy(weight_h.at[:, columns(start)], weight_v.at[k], weight_sem.at[k])

    weight_load(0).start()
    weight_load(1).start()
    table_loads = [
        pltpu.make_async_copy(src, dst, load_sem.at[2 + i])
        for i, (src, dst) in enumerate(
            ((fwd_high_h, fwd_high), (fwd_low_h, fwd_low), (inv_high_h, inv_high), (inv_low_h, inv_low))
        )
    ]
    part_loads = []
    for n in range(chunks):
        part_loads.append(pltpu.make_async_copy(keyed_h.at[:, pl.ds(n * step, step)], keyed_v.at[n], load_sem.at[6 + n]))
        part_loads.append(
            pltpu.make_async_copy(query_h.at[:, pl.ds(n * step, step)], query_v.at[n], load_sem.at[6 + chunks + n])
        )

    row, column, half = seq // (2 * edge), lax.rem(seq // 2, edge), lax.rem(seq, 2)

    def place(d):
        return (
            lax.rem(row + d // (2 * edge), edge) * edge + lax.rem(column + lax.rem(d // 2, edge), edge)
        ) * 2 + lax.rem(half + lax.rem(d, 2), 2)

    barrier = pltpu.get_barrier_semaphore()

    def greet(sem, peer, part):
        pl.semaphore_signal(sem, inc=1, device_id=(peer, part), device_id_type=MESH)

    for d in range(1, edge):
        greet(barrier, place(2 * d), proj)
        greet(barrier, place(2 * edge * d), proj)
    greet(barrier, place(1), proj)
    greet(barrier, seq, core_partner)
    greet(barrier, seq, chip_partner)

    def spread(source, target, send_sem, recv_sem):
        def send(d, carry):
            peer = place(d)
            pltpu.make_async_remote_copy(
                src_ref=source(peer), dst_ref=target(seq), send_sem=send_sem, recv_sem=recv_sem,
                device_id=(peer, proj), device_id_type=MESH,
            ).start()
            return carry

        pltpu.make_async_copy(source(seq), target(seq), recv_sem).start()
        lax.fori_loop(1, seq_count, send, 0)

    def await_bytes(ref, sem):
        pltpu.make_async_copy(ref, ref, sem).wait()

    token_load.wait()

    def near_copy(pair, n):
        return pltpu.make_async_remote_copy(
            src_ref=partial_v.at[2 * chunks * pair + 2 * n], dst_ref=near_recv.at[pair, n],
            send_sem=near_send_sem.at[pair, n], recv_sem=near_recv_sem.at[pair, n],
            device_id=(seq, core_partner), device_id_type=MESH,
        )

    def far_copy(n):
        return pltpu.make_async_remote_copy(
            src_ref=far_send.at[n], dst_ref=far_recv.at[n],
            send_sem=far_send_sem.at[n], recv_sem=far_recv_sem.at[n],
            device_id=(seq, chip_partner), device_id_type=MESH,
        )

    def sum_far(n):
        near_copy(0, n).wait_recv()
        far_send[n] = partial_v[2 * n + 1] + near_recv[0, n]

    def transpose_filters(n, carry):
        part = filters_v[:, columns(n * step)].T
        filt_send[:, pl.ds(n, 1)] = part.reshape(seq_count, 1, SUB, rows)
        return carry

    def project(k, carry):
        weight_load(k).wait()

        @pl.when(k + 2 < 4 * chunks)
        def _():
            weight_load(k + 2).start()

        partial_v[k] = dot(tokens_v[...], weight_v[k])

        @pl.when(k == 1)
        def _():
            filter_load.start()
            pl.semaphore_wait(barrier, 2 * edge + 1)
            near_copy(0, 0).start()
            for d in range(1, edge):
                greet(round_sem.at[0], place(2 * d), proj)

        first = k < 2 * chunks

        @pl.when(jnp.logical_and(jnp.logical_and(first, k >= 2), lax.rem(k, 2) == 0))
        def _():
            near_copy(0, k // 2).start()
            sum_far(k // 2 - 1)

            @pl.when(jnp.logical_or(EAGER, k <= 4))
            def _():
                far_copy(k // 2 - 1).start()

        @pl.when(k == 3)
        def _():
            pl.semaphore_wait(round_sem.at[0], edge - 1)
            greet(round_sem.at[1], place(1), proj)

        @pl.when(k == 5)
        def _():
            filter_load.wait()
            lax.fori_loop(0, chunks, transpose_filters, 0)
            pl.semaphore_wait(round_sem.at[1], 1)
            spread(lambda r: filt_send.at[r], lambda r: filt_recv.at[r], filt_send_sem, filt_recv_sem)
            for copy in table_loads + part_loads:
                copy.start()

        @pl.when(k == 2 * chunks)
        def _():
            sum_far(chunks - 1)

            @pl.when(EAGER)
            def _():
                far_copy(chunks - 1).start()

        @pl.when(jnp.logical_and(k >= 2 * chunks, lax.rem(k, 2) == 0))
        def _():
            near_copy(1, (k - 2 * chunks) // 2).start()

        return carry

    lax.fori_loop(0, 4 * chunks, project, 0)
    for copy in part_loads:
        copy.wait()

    def gate(n):
        near_copy(1, n).wait_recv()
        far_copy(n).wait_recv()
        valued = partial_v[2 * chunks + 2 * n + 1] + near_recv[1, n] + far_recv[n]
        gated = keyed_v[n].astype(F32) * valued
        gated_v[n] = gated
        sig_send[n] = gated.T.reshape(seq_count, SUB, rows)
        spread(
            lambda r: sig_send.at[n, r], lambda r: sig_recv.at[n, r], sig_send_sem.at[n], sig_recv_sem.at[n]
        )

    flip = (1 - 2 * lax.rem(lax.broadcasted_iota(jnp.int32, (1, 1, block), 2), 2)).astype(F32)

    def block_spectra(values):
        pairs = values.reshape(blocks, 2, SUB, rows)
        joined = jnp.concatenate([pairs[:, 0], pairs[:, 1]], axis=2).reshape(blocks * SUB, block)
        return table_dot(joined, fwd_high[...], fwd_low[...]).reshape(blocks, SUB, 2 * block)

    def filter_spectra(n, carry):
        spec = block_spectra(filt_recv[:, pl.ds(n, 1)].reshape(seq_count, SUB, rows))
        filt_spec[n] = spec
        filt_spec[n, 1:, :, :block] = spec[1:, :, :block] - flip * spec[:-1, :, block:]
        filt_spec[n, 1:, :, block:] = spec[1:, :, block:] + flip * spec[:-1, :, :block]
        return carry

    def all_filter_spectra():
        for copy in table_loads:
            copy.wait()
        await_bytes(filt_recv, filt_recv_sem)
        lax.fori_loop(0, chunks, filter_spectra, 0)

    def convolve(n):
        await_bytes(sig_recv.at[n], sig_recv_sem.at[n])
        sig_spec[...] = block_spectra(sig_recv[n])

        def lanes(part, carry):
            re = pl.ds(pl.multiple_of(part * 128, 128), 128)
            im = pl.ds(pl.multiple_of(block + part * 128, 128), 128)
            sig_re = [sig_spec[j, :, re] for j in range(blocks)]
            sig_im = [sig_spec[j, :, im] for j in range(blocks)]
            for s in range(blocks):
                sum_re = sum_im = None
                for j in range(s + 1):
                    tap_re, tap_im = filt_spec[n, j, :, re], filt_spec[n, j, :, im]
                    x_re, x_im = sig_re[s - j], sig_im[s - j]
                    term_re = tap_re * x_re - tap_im * x_im
                    term_im = tap_re * x_im + tap_im * x_re
                    sum_re = term_re if sum_re is None else sum_re + term_re
                    sum_im = term_im if sum_im is None else sum_im + term_im
                prod_spec[s, :, re] = sum_re
                prod_spec[s, :, im] = sum_im
            return carry

        lax.fori_loop(0, block // 128, lanes, 0)
        result = table_dot(
            prod_spec[...].reshape(blocks * SUB, 2 * block), inv_high[...], inv_low[...]
        ).reshape(blocks, SUB, block)
        pairs = jnp.stack([result[:, :, :rows], result[:, :, rows:]], axis=1)
        back_send[n] = pairs.reshape(seq_count, SUB, rows)
        spread(
            lambda r: back_send.at[n, r], lambda r: back_recv.at[n, r], back_send_sem.at[n], back_recv_sem.at[n]
        )

    def out_copy(n):
        return pltpu.make_async_copy(out_v.at[n], out_h.at[:, columns(n * step)], out_sem.at[n])

    def finish(n):
        await_bytes(back_recv.at[n], back_recv_sem.at[n])
        conv = back_recv[n].reshape(step, rows).T
        skip = skip_v[:, columns(n * step)]
        out_v[n] = (query_v[n].astype(F32) * (conv + skip * gated_v[n])).astype(BF16)
        out_copy(n).start()

    def stage(i, carry):
        @pl.when(i == SPEC_AT)
        def _():
            all_filter_spectra()

        @pl.when(i < chunks)
        def _():
            gate(i)

            @pl.when(jnp.logical_and(not EAGER, i + 2 < chunks))
            def _():
                far_copy(i + 2).start()

        @pl.when(i >= LAG)
        def _():
            convolve(i - LAG)

        return carry

    def finish_all(n, carry):
        finish(n)
        return carry

    lax.fori_loop(0, chunks + LAG, stage, 0)
    lax.fori_loop(0, chunks, finish_all, 0)

    def drain(n, carry):
        near_copy(0, n).wait_send()
        near_copy(1, n).wait_send()
        far_copy(n).wait_send()
        await_bytes(sig_send.at[n, pl.ds(0, seq_count - 1)], sig_send_sem.at[n])
        await_bytes(back_send.at[n, pl.ds(0, seq_count - 1)], back_send_sem.at[n])
        out_copy(n).wait()
        return carry

    await_bytes(filt_send.at[pl.ds(0, seq_count - 1)], filt_send_sem)
    lax.fori_loop(0, chunks, drain, 0)


def body(seq_count, tokens, value_weight, query, keyed, filters, skip_gain):
    rows, depth = tokens.shape
    width = skip_gain.shape[0]
    chunks = width // (seq_count * SUB)
    step = width // chunks
    block = 2 * rows
    blocks = seq_count // 2
    tables = [jnp.asarray(table) for table in odd_tables(block)]
    any_space = pl.BlockSpec(memory_space=pl.ANY)
    dma = pltpu.SemaphoreType.DMA
    strip = pltpu.VMEM((chunks, rows, step), F32)
    pieces = pltpu.VMEM((chunks, seq_count, SUB, rows), F32)
    filt_pieces = pltpu.VMEM((seq_count, chunks, SUB, rows), F32)
    return pl.pallas_call(
        functools.partial(kernel, math.isqrt(seq_count // 2), seq_count, chunks),
        out_shape=jax.ShapeDtypeStruct((rows, width), BF16),
        in_specs=[any_space] * 5 + [pl.BlockSpec(memory_space=pltpu.VMEM)] + [any_space] * 4,
        out_specs=any_space,
        scratch_shapes=[
            pltpu.VMEM((rows, depth), BF16),
            pltpu.VMEM((4 * chunks, depth, step), BF16),
            pltpu.VMEM((chunks, rows, step), BF16),
            pltpu.VMEM((chunks, rows, step), BF16),
            pltpu.VMEM((rows, width), F32),
            pltpu.VMEM((block, 2 * block), BF16),
            pltpu.VMEM((block, 2 * block), BF16),
            pltpu.VMEM((2 * block, block), BF16),
            pltpu.VMEM((2 * block, block), BF16),
            pltpu.VMEM((4 * chunks, rows, step), F32),
            pltpu.VMEM((2, chunks, rows, step), F32),
            strip, strip, strip,
            filt_pieces, filt_pieces, pieces, pieces, pieces, pieces,
            pltpu.VMEM((chunks, rows, step), BF16),
            pltpu.VMEM((chunks, blocks, SUB, 2 * block), F32),
            pltpu.VMEM((blocks, SUB, 2 * block), F32),
            pltpu.VMEM((blocks, SUB, 2 * block), F32),
            dma((6 + 2 * chunks,)), dma((4 * chunks,)),
            dma((2, chunks)), dma((2, chunks)), dma((chunks,)), dma((chunks,)),
            dma, dma, dma((chunks,)), dma((chunks,)), dma((chunks,)), dma((chunks,)), dma((chunks,)),
            pltpu.SemaphoreType.REGULAR((2,)),
        ],
        compiler_params=pltpu.CompilerParams(
            collective_id=0, has_side_effects=True, vmem_limit_bytes=56 * 1024 * 1024
        ),
    )(tokens, value_weight, query, keyed, filters, skip_gain.reshape(1, width), *tables)


def solution(mesh):
    in_specs = (
        P("seq", "proj"),
        P("proj", None),
        P("seq", "proj"),
        P("seq", "proj"),
        P("seq", "proj"),
        P("proj"),
    )
    return jax.shard_map(
        functools.partial(body, mesh.shape["seq"]), mesh=mesh, in_specs=in_specs, out_specs=P("seq", "proj"), check_vma=False
    )
```

```python
import functools
import math

import jax
import jax.numpy as jnp
import ml_dtypes
import numpy as np
from jax import lax
from jax.experimental import pallas as pl
from jax.experimental.pallas import tpu as pltpu
from jax.sharding import PartitionSpec as P

MESH = pl.DeviceIdType.MESH
F32 = jnp.float32
BF16 = jnp.bfloat16
SUB = 8
EAGER = False
SPEC_AT = 2
LAG = 3


def odd_tables(block):
    n = np.arange(block)
    k = np.arange(block)
    angle = np.pi / (2 * block) * ((n[:, None] * (2 * k[None, :] + 1)) % (4 * block))
    forward = np.concatenate([np.cos(angle), -np.sin(angle)], axis=1)
    inverse = forward.T / block

    def split(table):
        high = table.astype(np.float32).astype(ml_dtypes.bfloat16)
        low = (table - high.astype(np.float64)).astype(np.float32).astype(ml_dtypes.bfloat16)
        return high, low

    return split(forward) + split(inverse)


def split_rows(values):
    high = values.astype(BF16)
    low = (values - high.astype(F32)).astype(BF16)
    return high, low


def dot(a, b):
    return jnp.dot(a, b, preferred_element_type=F32)


def table_dot(values, table_high, table_low):
    rows = values.shape[0]
    high, low = split_rows(values)
    both = dot(jnp.concatenate([high, low], axis=0), table_high)
    return both[:rows] + both[rows:] + dot(high, table_low)


def kernel(
    edge, seq_count, chunks,
    tokens_h, weight_h, query_h, keyed_h, filters_h, skip_v, fwd_high_h, fwd_low_h, inv_high_h, inv_low_h,
    out_h,
    tokens_v, weight_v, query_v, keyed_v, filters_v, fwd_high, fwd_low, inv_high, inv_low,
    partial_v, near_recv, far_send, far_recv, gated_v,
    filt_send, filt_recv, sig_send, sig_recv, back_send, back_recv, out_v,
    filt_spec, sig_spec, prod_spec,
    load_sem, weight_sem, near_send_sem, near_recv_sem, far_send_sem, far_recv_sem,
    filt_send_sem, filt_recv_sem, sig_send_sem, sig_recv_sem, back_send_sem, back_recv_sem, out_sem, round_sem,
):
    seq = lax.axis_index("seq")
    proj = lax.axis_index("proj")
    core = lax.rem(proj, 2)
    side = proj // 2
    core_partner = side * 2 + 1 - core
    chip_partner = (1 - side) * 2 + core
    rows = tokens_h.shape[0]
    width = skip_v.shape[1]
    step = width // chunks
    blocks = seq_count // 2
    block = 2 * rows

    def columns(start):
        return pl.ds(pl.multiple_of(start, step), step)

    filter_load = pltpu.make_async_copy(filters_h, filters_v, load_sem.at[0])
    token_load = pltpu.make_async_copy(tokens_h, tokens_v, load_sem.at[1])
    token_load.start()

    def weight_load(k):
        pair, inner = k // (2 * chunks), lax.rem(k, 2 * chunks)
        home_side = side + (1 - pair) * (1 - 2 * side)
        home_core = core + (1 - lax.rem(inner, 2)) * (1 - 2 * core)
        start = (home_side * 2 + home_core) * width + inner // 2 * step
        return pltpu.make_async_copy(weight_h.at[:, columns(start)], weight_v.at[k], weight_sem.at[k])

    weight_load(0).start()
    weight_load(1).start()
    table_loads = [
        pltpu.make_async_copy(src, dst, load_sem.at[2 + i])
        for i, (src, dst) in enumerate(
            ((fwd_high_h, fwd_high), (fwd_low_h, fwd_low), (inv_high_h, inv_high), (inv_low_h, inv_low))
        )
    ]
    part_loads = []
    for n in range(chunks):
        part_loads.append(pltpu.make_async_copy(keyed_h.at[:, pl.ds(n * step, step)], keyed_v.at[n], load_sem.at[6 + n]))
        part_loads.append(
            pltpu.make_async_copy(query_h.at[:, pl.ds(n * step, step)], query_v.at[n], load_sem.at[6 + chunks + n])
        )

    row, column, half = seq // (2 * edge), lax.rem(seq // 2, edge), lax.rem(seq, 2)

    def place(d):
        return (
            lax.rem(row + d // (2 * edge), edge) * edge + lax.rem(column + lax.rem(d // 2, edge), edge)
        ) * 2 + lax.rem(half + lax.rem(d, 2), 2)

    barrier = pltpu.get_barrier_semaphore()

    def greet(sem, peer, part):
        pl.semaphore_signal(sem, inc=1, device_id=(peer, part), device_id_type=MESH)

    for d in range(1, edge):
        greet(barrier, place(2 * d), proj)
        greet(barrier, place(2 * edge * d), proj)
    greet(barrier, place(1), proj)
    greet(barrier, seq, core_partner)
    greet(barrier, seq, chip_partner)

    def spread(source, target, send_sem, recv_sem):
        def send(d, carry):
            peer = place(d)
            pltpu.make_async_remote_copy(
                src_ref=source(peer), dst_ref=target(seq), send_sem=send_sem, recv_sem=recv_sem,
                device_id=(peer, proj), device_id_type=MESH,
            ).start()
            return carry

        pltpu.make_async_copy(source(seq), target(seq), recv_sem).start()
        lax.fori_loop(1, seq_count, send, 0)

    def await_bytes(ref, sem):
        pltpu.make_async_copy(ref, ref, sem).wait()

    token_load.wait()

    def near_copy(pair, n):
        return pltpu.make_async_remote_copy(
            src_ref=partial_v.at[2 * chunks * pair + 2 * n], dst_ref=near_recv.at[pair, n],
            send_sem=near_send_sem.at[pair, n], recv_sem=near_recv_sem.at[pair, n],
            device_id=(seq, core_partner), device_id_type=MESH,
        )

    def far_copy(n):
        return pltpu.make_async_remote_copy(
            src_ref=far_send.at[n], dst_ref=far_recv.at[n],
            send_sem=far_send_sem.at[n], recv_sem=far_recv_sem.at[n],
            device_id=(seq, chip_partner), device_id_type=MESH,
        )

    def sum_far(n):
        near_copy(0, n).wait_recv()
        far_send[n] = partial_v[2 * n + 1] + near_recv[0, n]

    def transpose_filters(n, carry):
        part = filters_v[:, columns(n * step)].T
        filt_send[:, pl.ds(n, 1)] = part.reshape(seq_count, 1, SUB, rows)
        return carry

    def project(k, carry):
        weight_load(k).wait()

        @pl.when(2 * k + 3 < 4 * chunks)
        def _():
            weight_load(2 * k + 2).start()
            weight_load(2 * k + 3).start()

        partial_v[k] = dot(tokens_v[...], weight_v[k])

        @pl.when(k == 1)
        def _():
            filter_load.start()
            pl.semaphore_wait(barrier, 2 * edge + 1)
            near_copy(0, 0).start()
            for d in range(1, edge):
                greet(round_sem.at[0], place(2 * d), proj)

        first = k < 2 * chunks

        @pl.when(jnp.logical_and(jnp.logical_and(first, k >= 2), lax.rem(k, 2) == 0))
        def _():
            near_copy(0, k // 2).start()
            sum_far(k // 2 - 1)

            @pl.when(jnp.logical_or(EAGER, k <= 4))
            def _():
                far_copy(k // 2 - 1).start()

        @pl.when(k == 3)
        def _():
            pl.semaphore_wait(round_sem.at[0], edge - 1)
            greet(round_sem.at[1], place(1), proj)

        @pl.when(k == 5)
        def _():
            filter_load.wait()
            lax.fori_loop(0, chunks, transpose_filters, 0)
            pl.semaphore_wait(round_sem.at[1], 1)
            spread(lambda r: filt_send.at[r], lambda r: filt_recv.at[r], filt_send_sem, filt_recv_sem)
            for copy in table_loads + part_loads:
                copy.start()

        @pl.when(k == 2 * chunks)
        def _():
            sum_far(chunks - 1)

            @pl.when(EAGER)
            def _():
                far_copy(chunks - 1).start()

        @pl.when(jnp.logical_and(k >= 2 * chunks, lax.rem(k, 2) == 0))
        def _():
            near_copy(1, (k - 2 * chunks) // 2).start()

        return carry

    lax.fori_loop(0, 4 * chunks, project, 0)
    for copy in part_loads:
        copy.wait()

    def gate(n):
        near_copy(1, n).wait_recv()
        far_copy(n).wait_recv()
        valued = partial_v[2 * chunks + 2 * n + 1] + near_recv[1, n] + far_recv[n]
        gated = keyed_v[n].astype(F32) * valued
        gated_v[n] = gated
        sig_send[n] = gated.T.reshape(seq_count, SUB, rows)
        spread(
            lambda r: sig_send.at[n, r], lambda r: sig_recv.at[n, r], sig_send_sem.at[n], sig_recv_sem.at[n]
        )

    flip = (1 - 2 * lax.rem(lax.broadcasted_iota(jnp.int32, (1, 1, block), 2), 2)).astype(F32)

    def block_spectra(values):
        pairs = values.reshape(blocks, 2, SUB, rows)
        joined = jnp.concatenate([pairs[:, 0], pairs[:, 1]], axis=2).reshape(blocks * SUB, block)
        return table_dot(joined, fwd_high[...], fwd_low[...]).reshape(blocks, SUB, 2 * block)

    def filter_spectra(n, carry):
        spec = block_spectra(filt_recv[:, pl.ds(n, 1)].reshape(seq_count, SUB, rows))
        filt_spec[n] = spec
        filt_spec[n, 1:, :, :block] = spec[1:, :, :block] - flip * spec[:-1, :, block:]
        filt_spec[n, 1:, :, block:] = spec[1:, :, block:] + flip * spec[:-1, :, :block]
        return carry

    def all_filter_spectra():
        for copy in table_loads:
            copy.wait()
        await_bytes(filt_recv, filt_recv_sem)
        lax.fori_loop(0, chunks, filter_spectra, 0)

    def convolve(n):
        await_bytes(sig_recv.at[n], sig_recv_sem.at[n])
        sig_spec[...] = block_spectra(sig_recv[n])

        def lanes(part, carry):
            re = pl.ds(pl.multiple_of(part * 128, 128), 128)
            im = pl.ds(pl.multiple_of(block + part * 128, 128), 128)
            sig_re = [sig_spec[j, :, re] for j in range(blocks)]
            sig_im = [sig_spec[j, :, im] for j in range(blocks)]
            for s in range(blocks):
                sum_re = sum_im = None
                for j in range(s + 1):
                    tap_re, tap_im = filt_spec[n, j, :, re], filt_spec[n, j, :, im]
                    x_re, x_im = sig_re[s - j], sig_im[s - j]
                    term_re = tap_re * x_re - tap_im * x_im
                    term_im = tap_re * x_im + tap_im * x_re
                    sum_re = term_re if sum_re is None else sum_re + term_re
                    sum_im = term_im if sum_im is None else sum_im + term_im
                prod_spec[s, :, re] = sum_re
                prod_spec[s, :, im] = sum_im
            return carry

        lax.fori_loop(0, block // 128, lanes, 0)
        result = table_dot(
            prod_spec[...].reshape(blocks * SUB, 2 * block), inv_high[...], inv_low[...]
        ).reshape(blocks, SUB, block)
        pairs = jnp.stack([result[:, :, :rows], result[:, :, rows:]], axis=1)
        back_send[n] = pairs.reshape(seq_count, SUB, rows)
        spread(
            lambda r: back_send.at[n, r], lambda r: back_recv.at[n, r], back_send_sem.at[n], back_recv_sem.at[n]
        )

    def out_copy(n):
        return pltpu.make_async_copy(out_v.at[n], out_h.at[:, columns(n * step)], out_sem.at[n])

    def finish(n):
        await_bytes(back_recv.at[n], back_recv_sem.at[n])
        conv = back_recv[n].reshape(step, rows).T
        skip = skip_v[:, columns(n * step)]
        out_v[n] = (query_v[n].astype(F32) * (conv + skip * gated_v[n])).astype(BF16)
        out_copy(n).start()

    def stage(i, carry):
        @pl.when(i == SPEC_AT)
        def _():
            all_filter_spectra()

        @pl.when(i < chunks)
        def _():
            gate(i)

            @pl.when(jnp.logical_and(not EAGER, i + 2 < chunks))
            def _():
                far_copy(i + 2).start()

        @pl.when(i >= LAG)
        def _():
            convolve(i - LAG)

        return carry

    def finish_all(n, carry):
        finish(n)
        return carry

    lax.fori_loop(0, chunks + LAG, stage, 0)
    lax.fori_loop(0, chunks, finish_all, 0)

    def drain(n, carry):
        near_copy(0, n).wait_send()
        near_copy(1, n).wait_send()
        far_copy(n).wait_send()
        await_bytes(sig_send.at[n, pl.ds(0, seq_count - 1)], sig_send_sem.at[n])
        await_bytes(back_send.at[n, pl.ds(0, seq_count - 1)], back_send_sem.at[n])
        out_copy(n).wait()
        return carry

    await_bytes(filt_send.at[pl.ds(0, seq_count - 1)], filt_send_sem)
    lax.fori_loop(0, chunks, drain, 0)


def body(seq_count, tokens, value_weight, query, keyed, filters, skip_gain):
    rows, depth = tokens.shape
    width = skip_gain.shape[0]
    chunks = width // (seq_count * SUB)
    step = width // chunks
    block = 2 * rows
    blocks = seq_count // 2
    tables = [jnp.asarray(table) for table in odd_tables(block)]
    any_space = pl.BlockSpec(memory_space=pl.ANY)
    dma = pltpu.SemaphoreType.DMA
    strip = pltpu.VMEM((chunks, rows, step), F32)
    pieces = pltpu.VMEM((chunks, seq_count, SUB, rows), F32)
    filt_pieces = pltpu.VMEM((seq_count, chunks, SUB, rows), F32)
    return pl.pallas_call(
        functools.partial(kernel, math.isqrt(seq_count // 2), seq_count, chunks),
        out_shape=jax.ShapeDtypeStruct((rows, width), BF16),
        in_specs=[any_space] * 5 + [pl.BlockSpec(memory_space=pltpu.VMEM)] + [any_space] * 4,
        out_specs=any_space,
        scratch_shapes=[
            pltpu.VMEM((rows, depth), BF16),
            pltpu.VMEM((4 * chunks, depth, step), BF16),
            pltpu.VMEM((chunks, rows, step), BF16),
            pltpu.VMEM((chunks, rows, step), BF16),
            pltpu.VMEM((rows, width), F32),
            pltpu.VMEM((block, 2 * block), BF16),
            pltpu.VMEM((block, 2 * block), BF16),
            pltpu.VMEM((2 * block, block), BF16),
            pltpu.VMEM((2 * block, block), BF16),
            pltpu.VMEM((4 * chunks, rows, step), F32),
            pltpu.VMEM((2, chunks, rows, step), F32),
            strip, strip, strip,
            filt_pieces, filt_pieces, pieces, pieces, pieces, pieces,
            pltpu.VMEM((chunks, rows, step), BF16),
            pltpu.VMEM((chunks, blocks, SUB, 2 * block), F32),
            pltpu.VMEM((blocks, SUB, 2 * block), F32),
            pltpu.VMEM((blocks, SUB, 2 * block), F32),
            dma((6 + 2 * chunks,)), dma((4 * chunks,)),
            dma((2, chunks)), dma((2, chunks)), dma((chunks,)), dma((chunks,)),
            dma, dma, dma((chunks,)), dma((chunks,)), dma((chunks,)), dma((chunks,)), dma((chunks,)),
            pltpu.SemaphoreType.REGULAR((2,)),
        ],
        compiler_params=pltpu.CompilerParams(
            collective_id=0, has_side_effects=True, vmem_limit_bytes=56 * 1024 * 1024
        ),
    )(tokens, value_weight, query, keyed, filters, skip_gain.reshape(1, width), *tables)


def solution(mesh):
    in_specs = (
        P("seq", "proj"),
        P("proj", None),
        P("seq", "proj"),
        P("seq", "proj"),
        P("seq", "proj"),
        P("proj"),
    )
    return jax.shard_map(
        functools.partial(body, mesh.shape["seq"]), mesh=mesh, in_specs=in_specs, out_specs=P("seq", "proj"), check_vma=False
    )
```

```python
import functools
import math

import jax
import jax.numpy as jnp
import ml_dtypes
import numpy as np
from jax import lax
from jax.experimental import pallas as pl
from jax.experimental.pallas import tpu as pltpu
from jax.sharding import PartitionSpec as P

MESH = pl.DeviceIdType.MESH
F32 = jnp.float32
BF16 = jnp.bfloat16
SUB = 8
EAGER = False
SPEC_AT = 2
LAG = 2


def odd_tables(block):
    n = np.arange(block)
    k = np.arange(block)
    angle = np.pi / (2 * block) * ((n[:, None] * (2 * k[None, :] + 1)) % (4 * block))
    forward = np.concatenate([np.cos(angle), -np.sin(angle)], axis=1)
    inverse = forward.T / block

    def split(table):
        high = table.astype(np.float32).astype(ml_dtypes.bfloat16)
        low = (table - high.astype(np.float64)).astype(np.float32).astype(ml_dtypes.bfloat16)
        return high, low

    return split(forward) + split(inverse)


def split_rows(values):
    high = values.astype(BF16)
    low = (values - high.astype(F32)).astype(BF16)
    return high, low


def dot(a, b):
    return jnp.dot(a, b, preferred_element_type=F32)


def table_dot(values, table_high, table_low):
    rows = values.shape[0]
    high, low = split_rows(values)
    both = dot(jnp.concatenate([high, low], axis=0), table_high)
    return both[:rows] + both[rows:] + dot(high, table_low)


def kernel(
    edge, seq_count, chunks,
    tokens_h, weight_h, query_h, keyed_h, filters_h, skip_v, fwd_high_h, fwd_low_h, inv_high_h, inv_low_h,
    out_h,
    tokens_v, weight_v, query_v, keyed_v, filters_v, fwd_high, fwd_low, inv_high, inv_low,
    partial_v, near_recv, far_send, far_recv, gated_v,
    filt_send, filt_recv, sig_send, sig_recv, back_send, back_recv, out_v,
    filt_spec, sig_spec, prod_spec,
    load_sem, weight_sem, near_send_sem, near_recv_sem, far_send_sem, far_recv_sem,
    filt_send_sem, filt_recv_sem, sig_send_sem, sig_recv_sem, back_send_sem, back_recv_sem, out_sem, round_sem,
):
    seq = lax.axis_index("seq")
    proj = lax.axis_index("proj")
    core = lax.rem(proj, 2)
    side = proj // 2
    core_partner = side * 2 + 1 - core
    chip_partner = (1 - side) * 2 + core
    rows = tokens_h.shape[0]
    width = skip_v.shape[1]
    step = width // chunks
    blocks = seq_count // 2
    block = 2 * rows

    def columns(start):
        return pl.ds(pl.multiple_of(start, step), step)

    filter_load = pltpu.make_async_copy(filters_h, filters_v, load_sem.at[0])
    token_load = pltpu.make_async_copy(tokens_h, tokens_v, load_sem.at[1])
    token_load.start()

    def weight_load(k):
        pair, inner = k // (2 * chunks), lax.rem(k, 2 * chunks)
        home_side = side + (1 - pair) * (1 - 2 * side)
        home_core = core + (1 - lax.rem(inner, 2)) * (1 - 2 * core)
        start = (home_side * 2 + home_core) * width + inner // 2 * step
        return pltpu.make_async_copy(weight_h.at[:, columns(start)], weight_v.at[k], weight_sem.at[k])

    weight_load(0).start()
    weight_load(1).start()
    table_loads = [
        pltpu.make_async_copy(src, dst, load_sem.at[2 + i])
        for i, (src, dst) in enumerate(
            ((fwd_high_h, fwd_high), (fwd_low_h, fwd_low), (inv_high_h, inv_high), (inv_low_h, inv_low))
        )
    ]
    part_loads = []
    for n in range(chunks):
        part_loads.append(pltpu.make_async_copy(keyed_h.at[:, pl.ds(n * step, step)], keyed_v.at[n], load_sem.at[6 + n]))
        part_loads.append(
            pltpu.make_async_copy(query_h.at[:, pl.ds(n * step, step)], query_v.at[n], load_sem.at[6 + chunks + n])
        )

    row, column, half = seq // (2 * edge), lax.rem(seq // 2, edge), lax.rem(seq, 2)

    def place(d):
        return (
            lax.rem(row + d // (2 * edge), edge) * edge + lax.rem(column + lax.rem(d // 2, edge), edge)
        ) * 2 + lax.rem(half + lax.rem(d, 2), 2)

    barrier = pltpu.get_barrier_semaphore()

    def greet(sem, peer, part):
        pl.semaphore_signal(sem, inc=1, device_id=(peer, part), device_id_type=MESH)

    for d in range(1, edge):
        greet(barrier, place(2 * d), proj)
        greet(barrier, place(2 * edge * d), proj)
    greet(barrier, place(1), proj)
    greet(barrier, seq, core_partner)
    greet(barrier, seq, chip_partner)

    def spread(source, target, send_sem, recv_sem):
        def send(d, carry):
            peer = place(d)
            pltpu.make_async_remote_copy(
                src_ref=source(peer), dst_ref=target(seq), send_sem=send_sem, recv_sem=recv_sem,
                device_id=(peer, proj), device_id_type=MESH,
            ).start()
            return carry

        pltpu.make_async_copy(source(seq), target(seq), recv_sem).start()
        lax.fori_loop(1, seq_count, send, 0)

    def await_bytes(ref, sem):
        pltpu.make_async_copy(ref, ref, sem).wait()

    token_load.wait()

    def near_copy(pair, n):
        return pltpu.make_async_remote_copy(
            src_ref=partial_v.at[2 * chunks * pair + 2 * n], dst_ref=near_recv.at[pair, n],
            send_sem=near_send_sem.at[pair, n], recv_sem=near_recv_sem.at[pair, n],
            device_id=(seq, core_partner), device_id_type=MESH,
        )

    def far_copy(n):
        return pltpu.make_async_remote_copy(
            src_ref=far_send.at[n], dst_ref=far_recv.at[n],
            send_sem=far_send_sem.at[n], recv_sem=far_recv_sem.at[n],
            device_id=(seq, chip_partner), device_id_type=MESH,
        )

    def sum_far(n):
        near_copy(0, n).wait_recv()
        far_send[n] = partial_v[2 * n + 1] + near_recv[0, n]

    def transpose_filters(n, carry):
        part = filters_v[:, columns(n * step)].T
        filt_send[:, pl.ds(n, 1)] = part.reshape(seq_count, 1, SUB, rows)
        return carry

    def project(k, carry):
        weight_load(k).wait()

        @pl.when(2 * k + 3 < 4 * chunks)
        def _():
            weight_load(2 * k + 2).start()
            weight_load(2 * k + 3).start()

        partial_v[k] = dot(tokens_v[...], weight_v[k])

        @pl.when(k == 1)
        def _():
            filter_load.start()
            pl.semaphore_wait(barrier, 2 * edge + 1)
            near_copy(0, 0).start()
            for d in range(1, edge):
                greet(round_sem.at[0], place(2 * d), proj)

        first = k < 2 * chunks

        @pl.when(jnp.logical_and(jnp.logical_and(first, k >= 2), lax.rem(k, 2) == 0))
        def _():
            near_copy(0, k // 2).start()
            sum_far(k // 2 - 1)

            @pl.when(jnp.logical_or(EAGER, k <= 4))
            def _():
                far_copy(k // 2 - 1).start()

        @pl.when(k == 3)
        def _():
            pl.semaphore_wait(round_sem.at[0], edge - 1)
            greet(round_sem.at[1], place(1), proj)

        @pl.when(k == 5)
        def _():
            filter_load.wait()
            lax.fori_loop(0, chunks, transpose_filters, 0)
            pl.semaphore_wait(round_sem.at[1], 1)
            spread(lambda r: filt_send.at[r], lambda r: filt_recv.at[r], filt_send_sem, filt_recv_sem)
            for copy in table_loads + part_loads:
                copy.start()

        @pl.when(k == 2 * chunks)
        def _():
            sum_far(chunks - 1)

            @pl.when(EAGER)
            def _():
                far_copy(chunks - 1).start()

        @pl.when(jnp.logical_and(k >= 2 * chunks, lax.rem(k, 2) == 0))
        def _():
            near_copy(1, (k - 2 * chunks) // 2).start()

        return carry

    lax.fori_loop(0, 4 * chunks, project, 0)
    for copy in part_loads:
        copy.wait()

    def gate(n):
        near_copy(1, n).wait_recv()
        far_copy(n).wait_recv()
        valued = partial_v[2 * chunks + 2 * n + 1] + near_recv[1, n] + far_recv[n]
        gated = keyed_v[n].astype(F32) * valued
        gated_v[n] = gated
        sig_send[n] = gated.T.reshape(seq_count, SUB, rows)
        spread(
            lambda r: sig_send.at[n, r], lambda r: sig_recv.at[n, r], sig_send_sem.at[n], sig_recv_sem.at[n]
        )

    flip = (1 - 2 * lax.rem(lax.broadcasted_iota(jnp.int32, (1, 1, block), 2), 2)).astype(F32)

    def block_spectra(values):
        pairs = values.reshape(blocks, 2, SUB, rows)
        joined = jnp.concatenate([pairs[:, 0], pairs[:, 1]], axis=2).reshape(blocks * SUB, block)
        return table_dot(joined, fwd_high[...], fwd_low[...]).reshape(blocks, SUB, 2 * block)

    def filter_spectra(n, carry):
        spec = block_spectra(filt_recv[:, pl.ds(n, 1)].reshape(seq_count, SUB, rows))
        filt_spec[n] = spec
        filt_spec[n, 1:, :, :block] = spec[1:, :, :block] - flip * spec[:-1, :, block:]
        filt_spec[n, 1:, :, block:] = spec[1:, :, block:] + flip * spec[:-1, :, :block]
        return carry

    def all_filter_spectra():
        for copy in table_loads:
            copy.wait()
        await_bytes(filt_recv, filt_recv_sem)
        lax.fori_loop(0, chunks, filter_spectra, 0)

    def convolve(n):
        await_bytes(sig_recv.at[n], sig_recv_sem.at[n])
        sig_spec[...] = block_spectra(sig_recv[n])

        def lanes(part, carry):
            re = pl.ds(pl.multiple_of(part * 128, 128), 128)
            im = pl.ds(pl.multiple_of(block + part * 128, 128), 128)
            sig_re = [sig_spec[j, :, re] for j in range(blocks)]
            sig_im = [sig_spec[j, :, im] for j in range(blocks)]
            for s in range(blocks):
                sum_re = sum_im = None
                for j in range(s + 1):
                    tap_re, tap_im = filt_spec[n, j, :, re], filt_spec[n, j, :, im]
                    x_re, x_im = sig_re[s - j], sig_im[s - j]
                    term_re = tap_re * x_re - tap_im * x_im
                    term_im = tap_re * x_im + tap_im * x_re
                    sum_re = term_re if sum_re is None else sum_re + term_re
                    sum_im = term_im if sum_im is None else sum_im + term_im
                prod_spec[s, :, re] = sum_re
                prod_spec[s, :, im] = sum_im
            return carry

        lax.fori_loop(0, block // 128, lanes, 0)
        result = table_dot(
            prod_spec[...].reshape(blocks * SUB, 2 * block), inv_high[...], inv_low[...]
        ).reshape(blocks, SUB, block)
        pairs = jnp.stack([result[:, :, :rows], result[:, :, rows:]], axis=1)
        back_send[n] = pairs.reshape(seq_count, SUB, rows)
        spread(
            lambda r: back_send.at[n, r], lambda r: back_recv.at[n, r], back_send_sem.at[n], back_recv_sem.at[n]
        )

    def out_copy(n):
        return pltpu.make_async_copy(out_v.at[n], out_h.at[:, columns(n * step)], out_sem.at[n])

    def finish(n):
        await_bytes(back_recv.at[n], back_recv_sem.at[n])
        conv = back_recv[n].reshape(step, rows).T
        skip = skip_v[:, columns(n * step)]
        out_v[n] = (query_v[n].astype(F32) * (conv + skip * gated_v[n])).astype(BF16)
        out_copy(n).start()

    def stage(i, carry):
        @pl.when(i == SPEC_AT)
        def _():
            all_filter_spectra()

        @pl.when(i < chunks)
        def _():
            gate(i)

            @pl.when(jnp.logical_and(not EAGER, i + 2 < chunks))
            def _():
                far_copy(i + 2).start()

        @pl.when(i >= LAG)
        def _():
            convolve(i - LAG)

        return carry

    def finish_all(n, carry):
        finish(n)
        return carry

    lax.fori_loop(0, chunks + LAG, stage, 0)
    lax.fori_loop(0, chunks, finish_all, 0)

    def drain(n, carry):
        near_copy(0, n).wait_send()
        near_copy(1, n).wait_send()
        far_copy(n).wait_send()
        await_bytes(sig_send.at[n, pl.ds(0, seq_count - 1)], sig_send_sem.at[n])
        await_bytes(back_send.at[n, pl.ds(0, seq_count - 1)], back_send_sem.at[n])
        out_copy(n).wait()
        return carry

    await_bytes(filt_send.at[pl.ds(0, seq_count - 1)], filt_send_sem)
    lax.fori_loop(0, chunks, drain, 0)


def body(seq_count, tokens, value_weight, query, keyed, filters, skip_gain):
    rows, depth = tokens.shape
    width = skip_gain.shape[0]
    chunks = width // (seq_count * SUB)
    step = width // chunks
    block = 2 * rows
    blocks = seq_count // 2
    tables = [jnp.asarray(table) for table in odd_tables(block)]
    any_space = pl.BlockSpec(memory_space=pl.ANY)
    dma = pltpu.SemaphoreType.DMA
    strip = pltpu.VMEM((chunks, rows, step), F32)
    pieces = pltpu.VMEM((chunks, seq_count, SUB, rows), F32)
    filt_pieces = pltpu.VMEM((seq_count, chunks, SUB, rows), F32)
    return pl.pallas_call(
        functools.partial(kernel, math.isqrt(seq_count // 2), seq_count, chunks),
        out_shape=jax.ShapeDtypeStruct((rows, width), BF16),
        in_specs=[any_space] * 5 + [pl.BlockSpec(memory_space=pltpu.VMEM)] + [any_space] * 4,
        out_specs=any_space,
        scratch_shapes=[
            pltpu.VMEM((rows, depth), BF16),
            pltpu.VMEM((4 * chunks, depth, step), BF16),
            pltpu.VMEM((chunks, rows, step), BF16),
            pltpu.VMEM((chunks, rows, step), BF16),
            pltpu.VMEM((rows, width), F32),
            pltpu.VMEM((block, 2 * block), BF16),
            pltpu.VMEM((block, 2 * block), BF16),
            pltpu.VMEM((2 * block, block), BF16),
            pltpu.VMEM((2 * block, block), BF16),
            pltpu.VMEM((4 * chunks, rows, step), F32),
            pltpu.VMEM((2, chunks, rows, step), F32),
            strip, strip, strip,
            filt_pieces, filt_pieces, pieces, pieces, pieces, pieces,
            pltpu.VMEM((chunks, rows, step), BF16),
            pltpu.VMEM((chunks, blocks, SUB, 2 * block), F32),
            pltpu.VMEM((blocks, SUB, 2 * block), F32),
            pltpu.VMEM((blocks, SUB, 2 * block), F32),
            dma((6 + 2 * chunks,)), dma((4 * chunks,)),
            dma((2, chunks)), dma((2, chunks)), dma((chunks,)), dma((chunks,)),
            dma, dma, dma((chunks,)), dma((chunks,)), dma((chunks,)), dma((chunks,)), dma((chunks,)),
            pltpu.SemaphoreType.REGULAR((2,)),
        ],
        compiler_params=pltpu.CompilerParams(
            collective_id=0, has_side_effects=True, vmem_limit_bytes=56 * 1024 * 1024
        ),
    )(tokens, value_weight, query, keyed, filters, skip_gain.reshape(1, width), *tables)


def solution(mesh):
    in_specs = (
        P("seq", "proj"),
        P("proj", None),
        P("seq", "proj"),
        P("seq", "proj"),
        P("seq", "proj"),
        P("proj"),
    )
    return jax.shard_map(
        functools.partial(body, mesh.shape["seq"]), mesh=mesh, in_specs=in_specs, out_specs=P("seq", "proj"), check_vma=False
    )
```

```python
import functools
import math

import jax
import jax.numpy as jnp
import ml_dtypes
import numpy as np
from jax import lax
from jax.experimental import pallas as pl
from jax.experimental.pallas import tpu as pltpu
from jax.sharding import PartitionSpec as P

MESH = pl.DeviceIdType.MESH
F32 = jnp.float32
BF16 = jnp.bfloat16
SUB = 8
EAGER = False
SPEC_AT = 1
LAG = 1


def odd_tables(block):
    n = np.arange(block)
    k = np.arange(block)
    angle = np.pi / (2 * block) * ((n[:, None] * (2 * k[None, :] + 1)) % (4 * block))
    forward = np.concatenate([np.cos(angle), -np.sin(angle)], axis=1)
    inverse = forward.T / block

    def split(table):
        high = table.astype(np.float32).astype(ml_dtypes.bfloat16)
        low = (table - high.astype(np.float64)).astype(np.float32).astype(ml_dtypes.bfloat16)
        return high, low

    return split(forward) + split(inverse)


def split_rows(values):
    high = values.astype(BF16)
    low = (values - high.astype(F32)).astype(BF16)
    return high, low


def dot(a, b):
    return jnp.dot(a, b, preferred_element_type=F32)


def table_dot(values, table_high, table_low):
    rows = values.shape[0]
    high, low = split_rows(values)
    both = dot(jnp.concatenate([high, low], axis=0), table_high)
    return both[:rows] + both[rows:] + dot(high, table_low)


def kernel(
    edge, seq_count, chunks,
    tokens_h, weight_h, query_h, keyed_h, filters_h, skip_v, fwd_high_h, fwd_low_h, inv_high_h, inv_low_h,
    out_h,
    tokens_v, weight_v, query_v, keyed_v, filters_v, fwd_high, fwd_low, inv_high, inv_low,
    partial_v, near_recv, far_send, far_recv, gated_v,
    filt_send, filt_recv, sig_send, sig_recv, back_send, back_recv, out_v,
    filt_spec, sig_spec, prod_spec,
    load_sem, weight_sem, near_send_sem, near_recv_sem, far_send_sem, far_recv_sem,
    filt_send_sem, filt_recv_sem, sig_send_sem, sig_recv_sem, back_send_sem, back_recv_sem, out_sem, round_sem,
):
    seq = lax.axis_index("seq")
    proj = lax.axis_index("proj")
    core = lax.rem(proj, 2)
    side = proj // 2
    core_partner = side * 2 + 1 - core
    chip_partner = (1 - side) * 2 + core
    rows = tokens_h.shape[0]
    width = skip_v.shape[1]
    step = width // chunks
    blocks = seq_count // 2
    block = 2 * rows

    def columns(start):
        return pl.ds(pl.multiple_of(start, step), step)

    filter_load = pltpu.make_async_copy(filters_h, filters_v, load_sem.at[0])
    token_load = pltpu.make_async_copy(tokens_h, tokens_v, load_sem.at[1])
    token_load.start()

    def weight_load(k):
        pair, inner = k // (2 * chunks), lax.rem(k, 2 * chunks)
        home_side = side + (1 - pair) * (1 - 2 * side)
        home_core = core + (1 - lax.rem(inner, 2)) * (1 - 2 * core)
        start = (home_side * 2 + home_core) * width + inner // 2 * step
        return pltpu.make_async_copy(weight_h.at[:, columns(start)], weight_v.at[k], weight_sem.at[k])

    weight_load(0).start()
    weight_load(1).start()
    table_loads = [
        pltpu.make_async_copy(src, dst, load_sem.at[2 + i])
        for i, (src, dst) in enumerate(
            ((fwd_high_h, fwd_high), (fwd_low_h, fwd_low), (inv_high_h, inv_high), (inv_low_h, inv_low))
        )
    ]
    part_loads = []
    for n in range(chunks):
        part_loads.append(pltpu.make_async_copy(keyed_h.at[:, pl.ds(n * step, step)], keyed_v.at[n], load_sem.at[6 + n]))
        part_loads.append(
            pltpu.make_async_copy(query_h.at[:, pl.ds(n * step, step)], query_v.at[n], load_sem.at[6 + chunks + n])
        )

    row, column, half = seq // (2 * edge), lax.rem(seq // 2, edge), lax.rem(seq, 2)

    def place(d):
        return (
            lax.rem(row + d // (2 * edge), edge) * edge + lax.rem(column + lax.rem(d // 2, edge), edge)
        ) * 2 + lax.rem(half + lax.rem(d, 2), 2)

    barrier = pltpu.get_barrier_semaphore()

    def greet(sem, peer, part):
        pl.semaphore_signal(sem, inc=1, device_id=(peer, part), device_id_type=MESH)

    for d in range(1, edge):
        greet(barrier, place(2 * d), proj)
        greet(barrier, place(2 * edge * d), proj)
    greet(barrier, place(1), proj)
    greet(barrier, seq, core_partner)
    greet(barrier, seq, chip_partner)

    def spread(source, target, send_sem, recv_sem):
        def send(d, carry):
            peer = place(d)
            pltpu.make_async_remote_copy(
                src_ref=source(peer), dst_ref=target(seq), send_sem=send_sem, recv_sem=recv_sem,
                device_id=(peer, proj), device_id_type=MESH,
            ).start()
            return carry

        pltpu.make_async_copy(source(seq), target(seq), recv_sem).start()
        lax.fori_loop(1, seq_count, send, 0)

    def await_bytes(ref, sem):
        pltpu.make_async_copy(ref, ref, sem).wait()

    token_load.wait()

    def near_copy(pair, n):
        return pltpu.make_async_remote_copy(
            src_ref=partial_v.at[2 * chunks * pair + 2 * n], dst_ref=near_recv.at[pair, n],
            send_sem=near_send_sem.at[pair, n], recv_sem=near_recv_sem.at[pair, n],
            device_id=(seq, core_partner), device_id_type=MESH,
        )

    def far_copy(n):
        return pltpu.make_async_remote_copy(
            src_ref=far_send.at[n], dst_ref=far_recv.at[n],
            send_sem=far_send_sem.at[n], recv_sem=far_recv_sem.at[n],
            device_id=(seq, chip_partner), device_id_type=MESH,
        )

    def sum_far(n):
        near_copy(0, n).wait_recv()
        far_send[n] = partial_v[2 * n + 1] + near_recv[0, n]

    def transpose_filters(n, carry):
        part = filters_v[:, columns(n * step)].T
        filt_send[:, pl.ds(n, 1)] = part.reshape(seq_count, 1, SUB, rows)
        return carry

    def project(k, carry):
        weight_load(k).wait()

        @pl.when(2 * k + 3 < 4 * chunks)
        def _():
            weight_load(2 * k + 2).start()
            weight_load(2 * k + 3).start()

        partial_v[k] = dot(tokens_v[...], weight_v[k])

        @pl.when(k == 1)
        def _():
            filter_load.start()
            pl.semaphore_wait(barrier, 2 * edge + 1)
            near_copy(0, 0).start()
            for d in range(1, edge):
                greet(round_sem.at[0], place(2 * d), proj)

        first = k < 2 * chunks

        @pl.when(jnp.logical_and(jnp.logical_and(first, k >= 2), lax.rem(k, 2) == 0))
        def _():
            near_copy(0, k // 2).start()
            sum_far(k // 2 - 1)

            @pl.when(jnp.logical_or(EAGER, k <= 4))
            def _():
                far_copy(k // 2 - 1).start()

        @pl.when(k == 3)
        def _():
            pl.semaphore_wait(round_sem.at[0], edge - 1)
            greet(round_sem.at[1], place(1), proj)

        @pl.when(k == 5)
        def _():
            filter_load.wait()
            lax.fori_loop(0, chunks, transpose_filters, 0)
            pl.semaphore_wait(round_sem.at[1], 1)
            spread(lambda r: filt_send.at[r], lambda r: filt_recv.at[r], filt_send_sem, filt_recv_sem)
            for copy in table_loads + part_loads:
                copy.start()

        @pl.when(k == 2 * chunks)
        def _():
            sum_far(chunks - 1)

            @pl.when(EAGER)
            def _():
                far_copy(chunks - 1).start()

        @pl.when(jnp.logical_and(k >= 2 * chunks, lax.rem(k, 2) == 0))
        def _():
            near_copy(1, (k - 2 * chunks) // 2).start()

        return carry

    lax.fori_loop(0, 4 * chunks, project, 0)
    for copy in part_loads:
        copy.wait()

    def gate(n):
        near_copy(1, n).wait_recv()
        far_copy(n).wait_recv()
        valued = partial_v[2 * chunks + 2 * n + 1] + near_recv[1, n] + far_recv[n]
        gated = keyed_v[n].astype(F32) * valued
        gated_v[n] = gated
        sig_send[n] = gated.T.reshape(seq_count, SUB, rows)
        spread(
            lambda r: sig_send.at[n, r], lambda r: sig_recv.at[n, r], sig_send_sem.at[n], sig_recv_sem.at[n]
        )

    flip = (1 - 2 * lax.rem(lax.broadcasted_iota(jnp.int32, (1, 1, block), 2), 2)).astype(F32)

    def block_spectra(values):
        pairs = values.reshape(blocks, 2, SUB, rows)
        joined = jnp.concatenate([pairs[:, 0], pairs[:, 1]], axis=2).reshape(blocks * SUB, block)
        return table_dot(joined, fwd_high[...], fwd_low[...]).reshape(blocks, SUB, 2 * block)

    def filter_spectra(n, carry):
        spec = block_spectra(filt_recv[:, pl.ds(n, 1)].reshape(seq_count, SUB, rows))
        filt_spec[n] = spec
        filt_spec[n, 1:, :, :block] = spec[1:, :, :block] - flip * spec[:-1, :, block:]
        filt_spec[n, 1:, :, block:] = spec[1:, :, block:] + flip * spec[:-1, :, :block]
        return carry

    def all_filter_spectra():
        for copy in table_loads:
            copy.wait()
        await_bytes(filt_recv, filt_recv_sem)
        lax.fori_loop(0, chunks, filter_spectra, 0)

    def convolve(n):
        await_bytes(sig_recv.at[n], sig_recv_sem.at[n])
        sig_spec[...] = block_spectra(sig_recv[n])

        def lanes(part, carry):
            re = pl.ds(pl.multiple_of(part * 128, 128), 128)
            im = pl.ds(pl.multiple_of(block + part * 128, 128), 128)
            sig_re = [sig_spec[j, :, re] for j in range(blocks)]
            sig_im = [sig_spec[j, :, im] for j in range(blocks)]
            for s in range(blocks):
                sum_re = sum_im = None
                for j in range(s + 1):
                    tap_re, tap_im = filt_spec[n, j, :, re], filt_spec[n, j, :, im]
                    x_re, x_im = sig_re[s - j], sig_im[s - j]
                    term_re = tap_re * x_re - tap_im * x_im
                    term_im = tap_re * x_im + tap_im * x_re
                    sum_re = term_re if sum_re is None else sum_re + term_re
                    sum_im = term_im if sum_im is None else sum_im + term_im
                prod_spec[s, :, re] = sum_re
                prod_spec[s, :, im] = sum_im
            return carry

        lax.fori_loop(0, block // 128, lanes, 0)
        result = table_dot(
            prod_spec[...].reshape(blocks * SUB, 2 * block), inv_high[...], inv_low[...]
        ).reshape(blocks, SUB, block)
        pairs = jnp.stack([result[:, :, :rows], result[:, :, rows:]], axis=1)
        back_send[n] = pairs.reshape(seq_count, SUB, rows)
        spread(
            lambda r: back_send.at[n, r], lambda r: back_recv.at[n, r], back_send_sem.at[n], back_recv_sem.at[n]
        )

    def out_copy(n):
        return pltpu.make_async_copy(out_v.at[n], out_h.at[:, columns(n * step)], out_sem.at[n])

    def finish(n):
        await_bytes(back_recv.at[n], back_recv_sem.at[n])
        conv = back_recv[n].reshape(step, rows).T
        skip = skip_v[:, columns(n * step)]
        out_v[n] = (query_v[n].astype(F32) * (conv + skip * gated_v[n])).astype(BF16)
        out_copy(n).start()

    def stage(i, carry):
        @pl.when(i < chunks)
        def _():
            gate(i)

            @pl.when(jnp.logical_and(not EAGER, i + 2 < chunks))
            def _():
                far_copy(i + 2).start()

        @pl.when(i == SPEC_AT)
        def _():
            all_filter_spectra()

        @pl.when(i >= LAG)
        def _():
            convolve(i - LAG)

        return carry

    def finish_all(n, carry):
        finish(n)
        return carry

    lax.fori_loop(0, chunks + LAG, stage, 0)
    lax.fori_loop(0, chunks, finish_all, 0)

    def drain(n, carry):
        near_copy(0, n).wait_send()
        near_copy(1, n).wait_send()
        far_copy(n).wait_send()
        await_bytes(sig_send.at[n, pl.ds(0, seq_count - 1)], sig_send_sem.at[n])
        await_bytes(back_send.at[n, pl.ds(0, seq_count - 1)], back_send_sem.at[n])
        out_copy(n).wait()
        return carry

    await_bytes(filt_send.at[pl.ds(0, seq_count - 1)], filt_send_sem)
    lax.fori_loop(0, chunks, drain, 0)


def body(seq_count, tokens, value_weight, query, keyed, filters, skip_gain):
    rows, depth = tokens.shape
    width = skip_gain.shape[0]
    chunks = width // (seq_count * SUB)
    step = width // chunks
    block = 2 * rows
    blocks = seq_count // 2
    tables = [jnp.asarray(table) for table in odd_tables(block)]
    any_space = pl.BlockSpec(memory_space=pl.ANY)
    dma = pltpu.SemaphoreType.DMA
    strip = pltpu.VMEM((chunks, rows, step), F32)
    pieces = pltpu.VMEM((chunks, seq_count, SUB, rows), F32)
    filt_pieces = pltpu.VMEM((seq_count, chunks, SUB, rows), F32)
    return pl.pallas_call(
        functools.partial(kernel, math.isqrt(seq_count // 2), seq_count, chunks),
        out_shape=jax.ShapeDtypeStruct((rows, width), BF16),
        in_specs=[any_space] * 5 + [pl.BlockSpec(memory_space=pltpu.VMEM)] + [any_space] * 4,
        out_specs=any_space,
        scratch_shapes=[
            pltpu.VMEM((rows, depth), BF16),
            pltpu.VMEM((4 * chunks, depth, step), BF16),
            pltpu.VMEM((chunks, rows, step), BF16),
            pltpu.VMEM((chunks, rows, step), BF16),
            pltpu.VMEM((rows, width), F32),
            pltpu.VMEM((block, 2 * block), BF16),
            pltpu.VMEM((block, 2 * block), BF16),
            pltpu.VMEM((2 * block, block), BF16),
            pltpu.VMEM((2 * block, block), BF16),
            pltpu.VMEM((4 * chunks, rows, step), F32),
            pltpu.VMEM((2, chunks, rows, step), F32),
            strip, strip, strip,
            filt_pieces, filt_pieces, pieces, pieces, pieces, pieces,
            pltpu.VMEM((chunks, rows, step), BF16),
            pltpu.VMEM((chunks, blocks, SUB, 2 * block), F32),
            pltpu.VMEM((blocks, SUB, 2 * block), F32),
            pltpu.VMEM((blocks, SUB, 2 * block), F32),
            dma((6 + 2 * chunks,)), dma((4 * chunks,)),
            dma((2, chunks)), dma((2, chunks)), dma((chunks,)), dma((chunks,)),
            dma, dma, dma((chunks,)), dma((chunks,)), dma((chunks,)), dma((chunks,)), dma((chunks,)),
            pltpu.SemaphoreType.REGULAR((2,)),
        ],
        compiler_params=pltpu.CompilerParams(
            collective_id=0, has_side_effects=True, vmem_limit_bytes=56 * 1024 * 1024
        ),
    )(tokens, value_weight, query, keyed, filters, skip_gain.reshape(1, width), *tables)


def solution(mesh):
    in_specs = (
        P("seq", "proj"),
        P("proj", None),
        P("seq", "proj"),
        P("seq", "proj"),
        P("seq", "proj"),
        P("proj"),
    )
    return jax.shard_map(
        functools.partial(body, mesh.shape["seq"]), mesh=mesh, in_specs=in_specs, out_specs=P("seq", "proj"), check_vma=False
    )
```

```python
import functools
import math

import jax
import jax.numpy as jnp
import ml_dtypes
import numpy as np
from jax import lax
from jax.experimental import pallas as pl
from jax.experimental.pallas import tpu as pltpu
from jax.sharding import PartitionSpec as P

MESH = pl.DeviceIdType.MESH
F32 = jnp.float32
BF16 = jnp.bfloat16
SUB = 8
EAGER = False
SPEC_AT = 2
LAG = 2


def odd_tables(block):
    n = np.arange(block)
    k = np.arange(block)
    angle = np.pi / (2 * block) * ((n[:, None] * (2 * k[None, :] + 1)) % (4 * block))
    forward = np.concatenate([np.cos(angle), -np.sin(angle)], axis=1)
    inverse = forward.T / block

    def split(table):
        high = table.astype(np.float32).astype(ml_dtypes.bfloat16)
        low = (table - high.astype(np.float64)).astype(np.float32).astype(ml_dtypes.bfloat16)
        return high, low

    return split(forward) + split(inverse)


def split_rows(values):
    high = values.astype(BF16)
    low = (values - high.astype(F32)).astype(BF16)
    return high, low


def dot(a, b):
    return jnp.dot(a, b, preferred_element_type=F32)


def table_dot(values, table_high, table_low):
    rows = values.shape[0]
    high, low = split_rows(values)
    both = dot(jnp.concatenate([high, low], axis=0), table_high)
    return both[:rows] + both[rows:] + dot(high, table_low)


def kernel(
    edge, seq_count, chunks,
    tokens_h, weight_h, query_h, keyed_h, filters_h, skip_v, fwd_high_h, fwd_low_h, inv_high_h, inv_low_h,
    out_h,
    tokens_v, weight_v, query_v, keyed_v, filters_v, fwd_high, fwd_low, inv_high, inv_low,
    partial_v, near_recv, far_send, far_recv, gated_v,
    filt_send, filt_recv, sig_send, sig_recv, back_send, back_recv, out_v,
    filt_spec, sig_spec, prod_spec,
    load_sem, weight_sem, near_send_sem, near_recv_sem, far_send_sem, far_recv_sem,
    filt_send_sem, filt_recv_sem, sig_send_sem, sig_recv_sem, back_send_sem, back_recv_sem, out_sem, round_sem,
):
    seq = lax.axis_index("seq")
    proj = lax.axis_index("proj")
    core = lax.rem(proj, 2)
    side = proj // 2
    core_partner = side * 2 + 1 - core
    chip_partner = (1 - side) * 2 + core
    rows = tokens_h.shape[0]
    width = skip_v.shape[1]
    step = width // chunks
    blocks = seq_count // 2
    block = 2 * rows

    def columns(start):
        return pl.ds(pl.multiple_of(start, step), step)

    filter_load = pltpu.make_async_copy(filters_h, filters_v, load_sem.at[0])
    token_load = pltpu.make_async_copy(tokens_h, tokens_v, load_sem.at[1])
    token_load.start()

    def weight_load(k):
        pair, inner = k // (2 * chunks), lax.rem(k, 2 * chunks)
        home_side = side + (1 - pair) * (1 - 2 * side)
        home_core = core + (1 - lax.rem(inner, 2)) * (1 - 2 * core)
        start = (home_side * 2 + home_core) * width + inner // 2 * step
        return pltpu.make_async_copy(weight_h.at[:, columns(start)], weight_v.at[k], weight_sem.at[k])

    weight_load(0).start()
    weight_load(1).start()
    table_loads = [
        pltpu.make_async_copy(src, dst, load_sem.at[2 + i])
        for i, (src, dst) in enumerate(
            ((fwd_high_h, fwd_high), (fwd_low_h, fwd_low), (inv_high_h, inv_high), (inv_low_h, inv_low))
        )
    ]
    part_loads = []
    for n in range(chunks):
        part_loads.append(pltpu.make_async_copy(keyed_h.at[:, pl.ds(n * step, step)], keyed_v.at[n], load_sem.at[6 + n]))
        part_loads.append(
            pltpu.make_async_copy(query_h.at[:, pl.ds(n * step, step)], query_v.at[n], load_sem.at[6 + chunks + n])
        )

    row, column, half = seq // (2 * edge), lax.rem(seq // 2, edge), lax.rem(seq, 2)

    def place(d):
        return (
            lax.rem(row + d // (2 * edge), edge) * edge + lax.rem(column + lax.rem(d // 2, edge), edge)
        ) * 2 + lax.rem(half + lax.rem(d, 2), 2)

    barrier = pltpu.get_barrier_semaphore()

    def greet(sem, peer, part):
        pl.semaphore_signal(sem, inc=1, device_id=(peer, part), device_id_type=MESH)

    for d in range(1, edge):
        greet(barrier, place(2 * d), proj)
        greet(barrier, place(2 * edge * d), proj)
    greet(barrier, place(1), proj)
    greet(barrier, seq, core_partner)
    greet(barrier, seq, chip_partner)

    def spread(source, target, send_sem, recv_sem):
        def send(i, carry):
            peer = place(2 * i + 1 - i // (seq_count // 2) * (seq_count - 1))
            pltpu.make_async_remote_copy(
                src_ref=source(peer), dst_ref=target(seq), send_sem=send_sem, recv_sem=recv_sem,
                device_id=(peer, proj), device_id_type=MESH,
            ).start()
            return carry

        pltpu.make_async_copy(source(seq), target(seq), recv_sem).start()
        lax.fori_loop(0, seq_count - 1, send, 0)

    def await_bytes(ref, sem):
        pltpu.make_async_copy(ref, ref, sem).wait()

    token_load.wait()

    def near_copy(pair, n):
        return pltpu.make_async_remote_copy(
            src_ref=partial_v.at[2 * chunks * pair + 2 * n], dst_ref=near_recv.at[pair, n],
            send_sem=near_send_sem.at[pair, n], recv_sem=near_recv_sem.at[pair, n],
            device_id=(seq, core_partner), device_id_type=MESH,
        )

    def far_copy(n):
        return pltpu.make_async_remote_copy(
            src_ref=far_send.at[n], dst_ref=far_recv.at[n],
            send_sem=far_send_sem.at[n], recv_sem=far_recv_sem.at[n],
            device_id=(seq, chip_partner), device_id_type=MESH,
        )

    def sum_far(n):
        near_copy(0, n).wait_recv()
        far_send[n] = partial_v[2 * n + 1] + near_recv[0, n]

    def transpose_filters(n, carry):
        part = filters_v[:, columns(n * step)].T
        filt_send[:, pl.ds(n, 1)] = part.reshape(seq_count, 1, SUB, rows)
        return carry

    def project(k, carry):
        weight_load(k).wait()

        @pl.when(2 * k + 3 < 4 * chunks)
        def _():
            weight_load(2 * k + 2).start()
            weight_load(2 * k + 3).start()

        partial_v[k] = dot(tokens_v[...], weight_v[k])

        @pl.when(k == 1)
        def _():
            filter_load.start()
            pl.semaphore_wait(barrier, 2 * edge + 1)
            near_copy(0, 0).start()
            for d in range(1, edge):
                greet(round_sem.at[0], place(2 * d), proj)

        first = k < 2 * chunks

        @pl.when(jnp.logical_and(jnp.logical_and(first, k >= 2), lax.rem(k, 2) == 0))
        def _():
            near_copy(0, k // 2).start()
            sum_far(k // 2 - 1)

            @pl.when(jnp.logical_or(EAGER, k <= 4))
            def _():
                far_copy(k // 2 - 1).start()

        @pl.when(k == 3)
        def _():
            pl.semaphore_wait(round_sem.at[0], edge - 1)
            greet(round_sem.at[1], place(1), proj)

        @pl.when(k == 5)
        def _():
            filter_load.wait()
            lax.fori_loop(0, chunks, transpose_filters, 0)
            pl.semaphore_wait(round_sem.at[1], 1)
            spread(lambda r: filt_send.at[r], lambda r: filt_recv.at[r], filt_send_sem, filt_recv_sem)
            for copy in table_loads + part_loads:
                copy.start()

        @pl.when(k == 2 * chunks)
        def _():
            sum_far(chunks - 1)

            @pl.when(EAGER)
            def _():
                far_copy(chunks - 1).start()

        @pl.when(jnp.logical_and(k >= 2 * chunks, lax.rem(k, 2) == 0))
        def _():
            near_copy(1, (k - 2 * chunks) // 2).start()

        return carry

    lax.fori_loop(0, 4 * chunks, project, 0)
    for copy in part_loads:
        copy.wait()

    def gate(n):
        near_copy(1, n).wait_recv()
        far_copy(n).wait_recv()
        valued = partial_v[2 * chunks + 2 * n + 1] + near_recv[1, n] + far_recv[n]
        gated = keyed_v[n].astype(F32) * valued
        gated_v[n] = gated
        sig_send[n] = gated.T.reshape(seq_count, SUB, rows)
        spread(
            lambda r: sig_send.at[n, r], lambda r: sig_recv.at[n, r], sig_send_sem.at[n], sig_recv_sem.at[n]
        )

    flip = (1 - 2 * lax.rem(lax.broadcasted_iota(jnp.int32, (1, 1, block), 2), 2)).astype(F32)

    def block_spectra(values):
        pairs = values.reshape(blocks, 2, SUB, rows)
        joined = jnp.concatenate([pairs[:, 0], pairs[:, 1]], axis=2).reshape(blocks * SUB, block)
        return table_dot(joined, fwd_high[...], fwd_low[...]).reshape(blocks, SUB, 2 * block)

    def filter_spectra(n, carry):
        spec = block_spectra(filt_recv[:, pl.ds(n, 1)].reshape(seq_count, SUB, rows))
        filt_spec[n] = spec
        filt_spec[n, 1:, :, :block] = spec[1:, :, :block] - flip * spec[:-1, :, block:]
        filt_spec[n, 1:, :, block:] = spec[1:, :, block:] + flip * spec[:-1, :, :block]
        return carry

    def all_filter_spectra():
        for copy in table_loads:
            copy.wait()
        await_bytes(filt_recv, filt_recv_sem)
        lax.fori_loop(0, chunks, filter_spectra, 0)

    def convolve(n):
        await_bytes(sig_recv.at[n], sig_recv_sem.at[n])
        sig_spec[...] = block_spectra(sig_recv[n])

        def lanes(part, carry):
            re = pl.ds(pl.multiple_of(part * 128, 128), 128)
            im = pl.ds(pl.multiple_of(block + part * 128, 128), 128)
            sig_re = [sig_spec[j, :, re] for j in range(blocks)]
            sig_im = [sig_spec[j, :, im] for j in range(blocks)]
            for s in range(blocks):
                sum_re = sum_im = None
                for j in range(s + 1):
                    tap_re, tap_im = filt_spec[n, j, :, re], filt_spec[n, j, :, im]
                    x_re, x_im = sig_re[s - j], sig_im[s - j]
                    term_re = tap_re * x_re - tap_im * x_im
                    term_im = tap_re * x_im + tap_im * x_re
                    sum_re = term_re if sum_re is None else sum_re + term_re
                    sum_im = term_im if sum_im is None else sum_im + term_im
                prod_spec[s, :, re] = sum_re
                prod_spec[s, :, im] = sum_im
            return carry

        lax.fori_loop(0, block // 128, lanes, 0)
        result = table_dot(
            prod_spec[...].reshape(blocks * SUB, 2 * block), inv_high[...], inv_low[...]
        ).reshape(blocks, SUB, block)
        pairs = jnp.stack([result[:, :, :rows], result[:, :, rows:]], axis=1)
        back_send[n] = pairs.reshape(seq_count, SUB, rows)
        spread(
            lambda r: back_send.at[n, r], lambda r: back_recv.at[n, r], back_send_sem.at[n], back_recv_sem.at[n]
        )

    def out_copy(n):
        return pltpu.make_async_copy(out_v.at[n], out_h.at[:, columns(n * step)], out_sem.at[n])

    def finish(n):
        await_bytes(back_recv.at[n], back_recv_sem.at[n])
        conv = back_recv[n].reshape(step, rows).T
        skip = skip_v[:, columns(n * step)]
        out_v[n] = (query_v[n].astype(F32) * (conv + skip * gated_v[n])).astype(BF16)
        out_copy(n).start()

    def stage(i, carry):
        @pl.when(i == SPEC_AT)
        def _():
            all_filter_spectra()

        @pl.when(i < chunks)
        def _():
            gate(i)

            @pl.when(jnp.logical_and(not EAGER, i + 2 < chunks))
            def _():
                far_copy(i + 2).start()

        @pl.when(i >= LAG)
        def _():
            convolve(i - LAG)

        return carry

    def finish_all(n, carry):
        finish(n)
        return carry

    lax.fori_loop(0, chunks + LAG, stage, 0)
    lax.fori_loop(0, chunks, finish_all, 0)

    def drain(n, carry):
        near_copy(0, n).wait_send()
        near_copy(1, n).wait_send()
        far_copy(n).wait_send()
        await_bytes(sig_send.at[n, pl.ds(0, seq_count - 1)], sig_send_sem.at[n])
        await_bytes(back_send.at[n, pl.ds(0, seq_count - 1)], back_send_sem.at[n])
        out_copy(n).wait()
        return carry

    await_bytes(filt_send.at[pl.ds(0, seq_count - 1)], filt_send_sem)
    lax.fori_loop(0, chunks, drain, 0)


def body(seq_count, tokens, value_weight, query, keyed, filters, skip_gain):
    rows, depth = tokens.shape
    width = skip_gain.shape[0]
    chunks = width // (seq_count * SUB)
    step = width // chunks
    block = 2 * rows
    blocks = seq_count // 2
    tables = [jnp.asarray(table) for table in odd_tables(block)]
    any_space = pl.BlockSpec(memory_space=pl.ANY)
    dma = pltpu.SemaphoreType.DMA
    strip = pltpu.VMEM((chunks, rows, step), F32)
    pieces = pltpu.VMEM((chunks, seq_count, SUB, rows), F32)
    filt_pieces = pltpu.VMEM((seq_count, chunks, SUB, rows), F32)
    return pl.pallas_call(
        functools.partial(kernel, math.isqrt(seq_count // 2), seq_count, chunks),
        out_shape=jax.ShapeDtypeStruct((rows, width), BF16),
        in_specs=[any_space] * 5 + [pl.BlockSpec(memory_space=pltpu.VMEM)] + [any_space] * 4,
        out_specs=any_space,
        scratch_shapes=[
            pltpu.VMEM((rows, depth), BF16),
            pltpu.VMEM((4 * chunks, depth, step), BF16),
            pltpu.VMEM((chunks, rows, step), BF16),
            pltpu.VMEM((chunks, rows, step), BF16),
            pltpu.VMEM((rows, width), F32),
            pltpu.VMEM((block, 2 * block), BF16),
            pltpu.VMEM((block, 2 * block), BF16),
            pltpu.VMEM((2 * block, block), BF16),
            pltpu.VMEM((2 * block, block), BF16),
            pltpu.VMEM((4 * chunks, rows, step), F32),
            pltpu.VMEM((2, chunks, rows, step), F32),
            strip, strip, strip,
            filt_pieces, filt_pieces, pieces, pieces, pieces, pieces,
            pltpu.VMEM((chunks, rows, step), BF16),
            pltpu.VMEM((chunks, blocks, SUB, 2 * block), F32),
            pltpu.VMEM((blocks, SUB, 2 * block), F32),
            pltpu.VMEM((blocks, SUB, 2 * block), F32),
            dma((6 + 2 * chunks,)), dma((4 * chunks,)),
            dma((2, chunks)), dma((2, chunks)), dma((chunks,)), dma((chunks,)),
            dma, dma, dma((chunks,)), dma((chunks,)), dma((chunks,)), dma((chunks,)), dma((chunks,)),
            pltpu.SemaphoreType.REGULAR((2,)),
        ],
        compiler_params=pltpu.CompilerParams(
            collective_id=0, has_side_effects=True, vmem_limit_bytes=56 * 1024 * 1024
        ),
    )(tokens, value_weight, query, keyed, filters, skip_gain.reshape(1, width), *tables)


def solution(mesh):
    in_specs = (
        P("seq", "proj"),
        P("proj", None),
        P("seq", "proj"),
        P("seq", "proj"),
        P("seq", "proj"),
        P("proj"),
    )
    return jax.shard_map(
        functools.partial(body, mesh.shape["seq"]), mesh=mesh, in_specs=in_specs, out_specs=P("seq", "proj"), check_vma=False
    )
```

```python
import functools
import math

import jax
import jax.numpy as jnp
import ml_dtypes
import numpy as np
from jax import lax
from jax.experimental import pallas as pl
from jax.experimental.pallas import tpu as pltpu
from jax.sharding import PartitionSpec as P

MESH = pl.DeviceIdType.MESH
F32 = jnp.float32
BF16 = jnp.bfloat16
SUB = 8
EAGER = False
SPEC_AT = 2
LAG = 2


def odd_tables(block):
    n = np.arange(block)
    k = np.arange(block)
    angle = np.pi / (2 * block) * ((n[:, None] * (2 * k[None, :] + 1)) % (4 * block))
    forward = np.concatenate([np.cos(angle), -np.sin(angle)], axis=1)
    inverse = forward.T / block

    def split(table):
        high = table.astype(np.float32).astype(ml_dtypes.bfloat16)
        low = (table - high.astype(np.float64)).astype(np.float32).astype(ml_dtypes.bfloat16)
        return high, low

    return split(forward) + split(inverse)


def split_rows(values):
    high = values.astype(BF16)
    low = (values - high.astype(F32)).astype(BF16)
    return high, low


def dot(a, b):
    return jnp.dot(a, b, preferred_element_type=F32)


def table_dot(values, table_high, table_low):
    rows = values.shape[0]
    high, low = split_rows(values)
    both = dot(jnp.concatenate([high, low], axis=0), table_high)
    return both[:rows] + both[rows:] + dot(high, table_low)


def kernel(
    edge, seq_count, chunks,
    tokens_h, weight_h, query_h, keyed_h, filters_h, skip_v, fwd_high_h, fwd_low_h, inv_high_h, inv_low_h,
    out_h,
    tokens_v, weight_v, query_v, keyed_v, filters_v, fwd_high, fwd_low, inv_high, inv_low,
    partial_v, near_recv, far_send, far_recv, gated_v,
    filt_send, filt_recv, sig_send, sig_recv, back_send, back_recv, out_v,
    filt_spec, sig_spec, prod_spec,
    load_sem, weight_sem, near_send_sem, near_recv_sem, far_send_sem, far_recv_sem,
    filt_send_sem, filt_recv_sem, sig_send_sem, sig_recv_sem, back_send_sem, back_recv_sem, out_sem, round_sem,
):
    seq = lax.axis_index("seq")
    proj = lax.axis_index("proj")
    core = lax.rem(proj, 2)
    side = proj // 2
    core_partner = side * 2 + 1 - core
    chip_partner = (1 - side) * 2 + core
    rows = tokens_h.shape[0]
    width = skip_v.shape[1]
    step = width // chunks
    blocks = seq_count // 2
    block = 2 * rows

    def columns(start):
        return pl.ds(pl.multiple_of(start, step), step)

    filter_load = pltpu.make_async_copy(filters_h, filters_v, load_sem.at[0])
    token_load = pltpu.make_async_copy(tokens_h, tokens_v, load_sem.at[1])
    token_load.start()

    def weight_load(k):
        pair, inner = k // (2 * chunks), lax.rem(k, 2 * chunks)
        home_side = side + (1 - pair) * (1 - 2 * side)
        home_core = core + (1 - lax.rem(inner, 2)) * (1 - 2 * core)
        start = (home_side * 2 + home_core) * width + inner // 2 * step
        return pltpu.make_async_copy(weight_h.at[:, columns(start)], weight_v.at[k], weight_sem.at[k])

    weight_load(0).start()
    weight_load(1).start()
    table_loads = [
        pltpu.make_async_copy(src, dst, load_sem.at[2 + i])
        for i, (src, dst) in enumerate(
            ((fwd_high_h, fwd_high), (fwd_low_h, fwd_low), (inv_high_h, inv_high), (inv_low_h, inv_low))
        )
    ]
    part_loads = []
    for n in range(chunks):
        part_loads.append(pltpu.make_async_copy(keyed_h.at[:, pl.ds(n * step, step)], keyed_v.at[n], load_sem.at[6 + n]))
        part_loads.append(
            pltpu.make_async_copy(query_h.at[:, pl.ds(n * step, step)], query_v.at[n], load_sem.at[6 + chunks + n])
        )

    row, column, half = seq // (2 * edge), lax.rem(seq // 2, edge), lax.rem(seq, 2)

    def place(d):
        return (
            lax.rem(row + d // (2 * edge), edge) * edge + lax.rem(column + lax.rem(d // 2, edge), edge)
        ) * 2 + lax.rem(half + lax.rem(d, 2), 2)

    barrier = pltpu.get_barrier_semaphore()

    def greet(sem, peer, part):
        pl.semaphore_signal(sem, inc=1, device_id=(peer, part), device_id_type=MESH)

    for d in range(1, edge):
        greet(barrier, place(2 * d), proj)
        greet(barrier, place(2 * edge * d), proj)
    greet(barrier, place(1), proj)
    greet(barrier, seq, core_partner)
    greet(barrier, seq, chip_partner)

    def spread(source, target, send_sem, recv_sem):
        def send(i, carry):
            peer = place(2 * i + 1 - i // (seq_count // 2) * (seq_count - 1))
            pltpu.make_async_remote_copy(
                src_ref=source(peer), dst_ref=target(seq), send_sem=send_sem, recv_sem=recv_sem,
                device_id=(peer, proj), device_id_type=MESH,
            ).start()
            return carry

        lax.fori_loop(0, seq_count - 1, send, 0)
        pltpu.make_async_copy(source(seq), target(seq), recv_sem).start()

    def await_bytes(ref, sem):
        pltpu.make_async_copy(ref, ref, sem).wait()

    token_load.wait()

    def near_copy(pair, n):
        return pltpu.make_async_remote_copy(
            src_ref=partial_v.at[2 * chunks * pair + 2 * n], dst_ref=near_recv.at[pair, n],
            send_sem=near_send_sem.at[pair, n], recv_sem=near_recv_sem.at[pair, n],
            device_id=(seq, core_partner), device_id_type=MESH,
        )

    def far_copy(n):
        return pltpu.make_async_remote_copy(
            src_ref=far_send.at[n], dst_ref=far_recv.at[n],
            send_sem=far_send_sem.at[n], recv_sem=far_recv_sem.at[n],
            device_id=(seq, chip_partner), device_id_type=MESH,
        )

    def sum_far(n):
        near_copy(0, n).wait_recv()
        far_send[n] = partial_v[2 * n + 1] + near_recv[0, n]

    def transpose_filters(n, carry):
        part = filters_v[:, columns(n * step)].T
        filt_send[:, pl.ds(n, 1)] = part.reshape(seq_count, 1, SUB, rows)
        return carry

    def project(k, carry):
        weight_load(k).wait()

        @pl.when(2 * k + 3 < 4 * chunks)
        def _():
            weight_load(2 * k + 2).start()
            weight_load(2 * k + 3).start()

        partial_v[k] = dot(tokens_v[...], weight_v[k])

        @pl.when(k == 1)
        def _():
            filter_load.start()
            pl.semaphore_wait(barrier, 2 * edge + 1)
            near_copy(0, 0).start()
            for d in range(1, edge):
                greet(round_sem.at[0], place(2 * d), proj)

        first = k < 2 * chunks

        @pl.when(jnp.logical_and(jnp.logical_and(first, k >= 2), lax.rem(k, 2) == 0))
        def _():
            near_copy(0, k // 2).start()
            sum_far(k // 2 - 1)

            @pl.when(jnp.logical_or(EAGER, k <= 4))
            def _():
                far_copy(k // 2 - 1).start()

        @pl.when(k == 3)
        def _():
            pl.semaphore_wait(round_sem.at[0], edge - 1)
            greet(round_sem.at[1], place(1), proj)

        @pl.when(k == 5)
        def _():
            filter_load.wait()
            lax.fori_loop(0, chunks, transpose_filters, 0)
            pl.semaphore_wait(round_sem.at[1], 1)
            spread(lambda r: filt_send.at[r], lambda r: filt_recv.at[r], filt_send_sem, filt_recv_sem)
            for copy in table_loads + part_loads:
                copy.start()

        @pl.when(k == 2 * chunks)
        def _():
            sum_far(chunks - 1)

            @pl.when(EAGER)
            def _():
                far_copy(chunks - 1).start()

        @pl.when(jnp.logical_and(k >= 2 * chunks, lax.rem(k, 2) == 0))
        def _():
            near_copy(1, (k - 2 * chunks) // 2).start()

        return carry

    lax.fori_loop(0, 4 * chunks, project, 0)
    for copy in part_loads:
        copy.wait()

    def gate(n):
        near_copy(1, n).wait_recv()
        far_copy(n).wait_recv()
        valued = partial_v[2 * chunks + 2 * n + 1] + near_recv[1, n] + far_recv[n]
        gated = keyed_v[n].astype(F32) * valued
        sig_send[n] = gated.T.reshape(seq_count, SUB, rows)
        spread(
            lambda r: sig_send.at[n, r], lambda r: sig_recv.at[n, r], sig_send_sem.at[n], sig_recv_sem.at[n]
        )
        gated_v[n] = gated

    flip = (1 - 2 * lax.rem(lax.broadcasted_iota(jnp.int32, (1, 1, block), 2), 2)).astype(F32)

    def block_spectra(values):
        pairs = values.reshape(blocks, 2, SUB, rows)
        joined = jnp.concatenate([pairs[:, 0], pairs[:, 1]], axis=2).reshape(blocks * SUB, block)
        return table_dot(joined, fwd_high[...], fwd_low[...]).reshape(blocks, SUB, 2 * block)

    def filter_spectra(n, carry):
        spec = block_spectra(filt_recv[:, pl.ds(n, 1)].reshape(seq_count, SUB, rows))
        filt_spec[n] = spec
        filt_spec[n, 1:, :, :block] = spec[1:, :, :block] - flip * spec[:-1, :, block:]
        filt_spec[n, 1:, :, block:] = spec[1:, :, block:] + flip * spec[:-1, :, :block]
        return carry

    def all_filter_spectra():
        for copy in table_loads:
            copy.wait()
        await_bytes(filt_recv, filt_recv_sem)
        lax.fori_loop(0, chunks, filter_spectra, 0)

    def convolve(n):
        await_bytes(sig_recv.at[n], sig_recv_sem.at[n])
        sig_spec[...] = block_spectra(sig_recv[n])

        def lanes(part, carry):
            re = pl.ds(pl.multiple_of(part * 128, 128), 128)
            im = pl.ds(pl.multiple_of(block + part * 128, 128), 128)
            sig_re = [sig_spec[j, :, re] for j in range(blocks)]
            sig_im = [sig_spec[j, :, im] for j in range(blocks)]
            for s in range(blocks):
                sum_re = sum_im = None
                for j in range(s + 1):
                    tap_re, tap_im = filt_spec[n, j, :, re], filt_spec[n, j, :, im]
                    x_re, x_im = sig_re[s - j], sig_im[s - j]
                    term_re = tap_re * x_re - tap_im * x_im
                    term_im = tap_re * x_im + tap_im * x_re
                    sum_re = term_re if sum_re is None else sum_re + term_re
                    sum_im = term_im if sum_im is None else sum_im + term_im
                prod_spec[s, :, re] = sum_re
                prod_spec[s, :, im] = sum_im
            return carry

        lax.fori_loop(0, block // 128, lanes, 0)
        result = table_dot(
            prod_spec[...].reshape(blocks * SUB, 2 * block), inv_high[...], inv_low[...]
        ).reshape(blocks, SUB, block)
        pairs = jnp.stack([result[:, :, :rows], result[:, :, rows:]], axis=1)
        back_send[n] = pairs.reshape(seq_count, SUB, rows)
        spread(
            lambda r: back_send.at[n, r], lambda r: back_recv.at[n, r], back_send_sem.at[n], back_recv_sem.at[n]
        )

    def out_copy(n):
        return pltpu.make_async_copy(out_v.at[n], out_h.at[:, columns(n * step)], out_sem.at[n])

    def finish(n):
        await_bytes(back_recv.at[n], back_recv_sem.at[n])
        conv = back_recv[n].reshape(step, rows).T
        skip = skip_v[:, columns(n * step)]
        out_v[n] = (query_v[n].astype(F32) * (conv + skip * gated_v[n])).astype(BF16)
        out_copy(n).start()

    def stage(i, carry):
        @pl.when(i == SPEC_AT)
        def _():
            all_filter_spectra()

        @pl.when(i < chunks)
        def _():
            gate(i)

            @pl.when(jnp.logical_and(not EAGER, i + 2 < chunks))
            def _():
                far_copy(i + 2).start()

        @pl.when(i >= LAG)
        def _():
            convolve(i - LAG)

        return carry

    def finish_all(n, carry):
        finish(n)
        return carry

    lax.fori_loop(0, chunks + LAG, stage, 0)
    lax.fori_loop(0, chunks, finish_all, 0)

    def drain(n, carry):
        near_copy(0, n).wait_send()
        near_copy(1, n).wait_send()
        far_copy(n).wait_send()
        await_bytes(sig_send.at[n, pl.ds(0, seq_count - 1)], sig_send_sem.at[n])
        await_bytes(back_send.at[n, pl.ds(0, seq_count - 1)], back_send_sem.at[n])
        out_copy(n).wait()
        return carry

    await_bytes(filt_send.at[pl.ds(0, seq_count - 1)], filt_send_sem)
    lax.fori_loop(0, chunks, drain, 0)


def body(seq_count, tokens, value_weight, query, keyed, filters, skip_gain):
    rows, depth = tokens.shape
    width = skip_gain.shape[0]
    chunks = width // (seq_count * SUB)
    step = width // chunks
    block = 2 * rows
    blocks = seq_count // 2
    tables = [jnp.asarray(table) for table in odd_tables(block)]
    any_space = pl.BlockSpec(memory_space=pl.ANY)
    dma = pltpu.SemaphoreType.DMA
    strip = pltpu.VMEM((chunks, rows, step), F32)
    pieces = pltpu.VMEM((chunks, seq_count, SUB, rows), F32)
    filt_pieces = pltpu.VMEM((seq_count, chunks, SUB, rows), F32)
    return pl.pallas_call(
        functools.partial(kernel, math.isqrt(seq_count // 2), seq_count, chunks),
        out_shape=jax.ShapeDtypeStruct((rows, width), BF16),
        in_specs=[any_space] * 5 + [pl.BlockSpec(memory_space=pltpu.VMEM)] + [any_space] * 4,
        out_specs=any_space,
        scratch_shapes=[
            pltpu.VMEM((rows, depth), BF16),
            pltpu.VMEM((4 * chunks, depth, step), BF16),
            pltpu.VMEM((chunks, rows, step), BF16),
            pltpu.VMEM((chunks, rows, step), BF16),
            pltpu.VMEM((rows, width), F32),
            pltpu.VMEM((block, 2 * block), BF16),
            pltpu.VMEM((block, 2 * block), BF16),
            pltpu.VMEM((2 * block, block), BF16),
            pltpu.VMEM((2 * block, block), BF16),
            pltpu.VMEM((4 * chunks, rows, step), F32),
            pltpu.VMEM((2, chunks, rows, step), F32),
            strip, strip, strip,
            filt_pieces, filt_pieces, pieces, pieces, pieces, pieces,
            pltpu.VMEM((chunks, rows, step), BF16),
            pltpu.VMEM((chunks, blocks, SUB, 2 * block), F32),
            pltpu.VMEM((blocks, SUB, 2 * block), F32),
            pltpu.VMEM((blocks, SUB, 2 * block), F32),
            dma((6 + 2 * chunks,)), dma((4 * chunks,)),
            dma((2, chunks)), dma((2, chunks)), dma((chunks,)), dma((chunks,)),
            dma, dma, dma((chunks,)), dma((chunks,)), dma((chunks,)), dma((chunks,)), dma((chunks,)),
            pltpu.SemaphoreType.REGULAR((2,)),
        ],
        compiler_params=pltpu.CompilerParams(
            collective_id=0, has_side_effects=True, vmem_limit_bytes=56 * 1024 * 1024
        ),
    )(tokens, value_weight, query, keyed, filters, skip_gain.reshape(1, width), *tables)


def solution(mesh):
    in_specs = (
        P("seq", "proj"),
        P("proj", None),
        P("seq", "proj"),
        P("seq", "proj"),
        P("seq", "proj"),
        P("proj"),
    )
    return jax.shard_map(
        functools.partial(body, mesh.shape["seq"]), mesh=mesh, in_specs=in_specs, out_specs=P("seq", "proj"), check_vma=False
    )
```
